512 devices in a mesh: row: 16 (over y, x), col: 32 (over z, core).
Axes of the slice: x: 4, y: 4, z: 16, core: 2. Of those that a mesh axis runs over, the one named last changes fastest.
Arguments:
- right_sides: float32 [4, 16, 64, 64, 128], P(None, 'row', 'col'), may hold values from -6 to 6
- inverse_blocks: float32 [4, 16, 64, 128, 128], P(None, 'row', 'col')
- coupling_blocks: float32 [3, 16, 512, 128, 128], P(None, 'row', 'col'), may hold values from -0.25 to 0.25
- slot_counts: int32 [4, 16, 32], P(None, 'row', 'col'), may hold values from 1 to 2, as said below
- edge_sources: int32 [3, 16, 512], P(None, 'row', 'col'), may hold values from -1 to 191, as said below
- edge_targets: int32 [3, 16, 512], P(None, 'row', 'col'), may hold values from -1 to 31, as said below
Outputs:
- solution: float32 [4, 16, 64, 64, 128], P(None, 'row', 'col')
The draws below stay inside these ranges and needn't reach their ends.
Inputs may be any that keep to these rules, and one draw needn't show every extreme that they name: `slot_counts`: at every level some device holds 2 live slots. `edge_sources`: for the 16 slots of one device at level l + 1 (l the first index): used slots come first and hold m * 32 * 2 + p, a live slot (m, this device row, p) with m <= l; unused slots hold -1; at every level some device uses all 16. `edge_targets`: -1 exactly where edge_sources is -1; else r * 2 + s, where slot (l + 1, r, c * 2 + s) is live and c is this device's column.
All inputs are finite; a program needn't handle non-finite values.
Results may differ from the reference program's by a relative error of at most 0.0001.
Values sent between devices are 32-bit elements; how exact they have to be, the bound alone decides.
No kernel may reach another device: no remote copies, remote signals or barrier semaphores. Data moves between devices by JAX's collectives and lax.ppermute only.
A program may use at most 64 MiB of HBM per device.

```python
import math
import jax
import jax.numpy as jnp
from jax import lax

B = 128
R = 64
LEVELS = 4
DSLOT = 2
EDGES = 16
N_ROW = 16
N_COL = 32


def layout(key):
    subkeys = jax.random.split(key, 9)
    cell_ids = jnp.arange(N_ROW * N_COL, dtype=jnp.int32).reshape(N_ROW, N_COL)
    last_cell = N_ROW * N_COL - 1
    counts = jax.random.randint(subkeys[0], (LEVELS, N_ROW, N_COL), 1, DSLOT + 1)
    chosen = jax.random.randint(subkeys[1], (LEVELS,), 0, N_ROW * N_COL)
    counts = jnp.where(cell_ids[None] == chosen[:, None, None], DSLOT, counts)
    counts = jnp.where(cell_ids[None] == last_cell, DSLOT, counts).astype(jnp.int32)
    grid_shape = (LEVELS - 1, N_ROW, N_COL, EDGES)
    edge_used = jax.random.randint(subkeys[2], (LEVELS - 1, N_ROW, N_COL), 0, EDGES + 1)
    chosen_full = jax.random.randint(subkeys[3], (LEVELS - 1,), 0, N_ROW * N_COL)
    chosen_full = chosen_full.at[LEVELS - 2].set(last_cell)
    edge_used = jnp.where(cell_ids[None] == chosen_full[:, None, None], EDGES, edge_used)
    level_ids = jnp.arange(1, LEVELS, dtype=jnp.int32)[:, None, None, None]
    row_ids = jnp.arange(N_ROW, dtype=jnp.int32)[None, :, None, None]
    col_ids = jnp.arange(N_COL, dtype=jnp.int32)[None, None, :, None]
    src_level = jax.random.randint(subkeys[4], grid_shape, 0, jnp.broadcast_to(level_ids, grid_shape))
    src_col = jax.random.randint(subkeys[5], grid_shape, 0, N_COL)
    src_count = counts[src_level, jnp.broadcast_to(row_ids, grid_shape), src_col]
    src_slot = jax.random.randint(subkeys[6], grid_shape, 0, src_count)
    sources = src_level * (N_COL * DSLOT) + src_col * DSLOT + src_slot
    dst_row = jax.random.randint(subkeys[7], grid_shape, 0, N_ROW)
    dst_count = counts[jnp.broadcast_to(level_ids, grid_shape), dst_row, jnp.broadcast_to(col_ids, grid_shape)]
    dst_slot = jax.random.randint(subkeys[8], grid_shape, 0, dst_count)
    targets = dst_row * DSLOT + dst_slot
    sources = sources.at[LEVELS - 2, N_ROW - 1, N_COL - 1, 0].set((LEVELS - 1) * N_COL * DSLOT - 1)
    targets = targets.at[LEVELS - 2, N_ROW - 1, N_COL - 1, 0].set(N_ROW * DSLOT - 1)
    active = jnp.arange(EDGES, dtype=jnp.int32)[None, None, None, :] < edge_used[..., None]
    sources = jnp.where(active, sources, -1).astype(jnp.int32).reshape(LEVELS - 1, N_ROW, N_COL * EDGES)
    targets = jnp.where(active, targets, -1).astype(jnp.int32).reshape(LEVELS - 1, N_ROW, N_COL * EDGES)
    return (counts, sources, targets)


def draw_slot_counts(key, part):
    return layout(key)[0]


def draw_edge_sources(key, part):
    return layout(key)[1]


def draw_edge_targets(key, part):
    return layout(key)[2]


def draw_inverse_blocks(key, part):
    key = jax.random.fold_in(key, 11)
    subkeys = jax.random.split(key, 2)
    grid_shape = (LEVELS, N_ROW, N_COL * DSLOT)
    diagonal = jax.random.uniform(subkeys[0], grid_shape + (B,), jnp.float32, 0.6, 1.6)
    offdiag = jax.random.normal(subkeys[1], grid_shape + (B, B), jnp.float32) * (0.4 / math.sqrt(B))
    return offdiag + diagonal[..., None] * jnp.eye(B, dtype=jnp.float32)


def level_of(key, dims, cuts, low, high):
    def one(axis_at, parts):
        heights = jax.random.uniform(jax.random.fold_in(jax.random.fold_in(key, 6), axis_at), (parts,), jnp.float32, low / len(cuts), high / len(cuts))
        return jnp.repeat(jnp.exp(heights), dims[axis_at] // parts).reshape((-1,) + (1,) * (len(dims) - axis_at - 1))

    level = one(*cuts[0])
    for cut in cuts[1:]:
        level = level * one(*cut)
    return level


def noise(stream_key, extent, scale, reach, cuts=(), kind=jnp.bfloat16):
    values = scale * jax.random.normal(stream_key, extent, jnp.float32)
    if cuts:
        values = values * level_of(stream_key, extent, cuts, -0.22, 0.18)
    return jnp.clip(values, -reach, reach).astype(kind)


def setup_inputs(seed: int = 0) -> dict:
    streams_of = jax.random.split(jax.random.key(seed), 7)
    return {
        "right_sides": noise(streams_of[0], (LEVELS, N_ROW, N_COL * DSLOT, R, B), 1.0, 6.0, ((1, 16), (2, 32)), jnp.float32),
        "inverse_blocks": draw_inverse_blocks(jax.random.fold_in(streams_of[6], 71), 0),
        "coupling_blocks": noise(streams_of[2], (LEVELS - 1, N_ROW, N_COL * EDGES, B, B), (4 * B) ** -0.5, 0.25, ((1, 16), (2, 32)), jnp.float32),
        "slot_counts": draw_slot_counts(jax.random.fold_in(streams_of[6], 71), 0),
        "edge_sources": draw_edge_sources(jax.random.fold_in(streams_of[6], 71), 0),
        "edge_targets": draw_edge_targets(jax.random.fold_in(streams_of[6], 71), 0),
    }


def reference(right_sides, inverse_blocks, coupling_blocks, slot_counts, edge_sources, edge_targets):
    row_span = N_COL * DSLOT
    levels_done = []
    row_ids = jnp.arange(N_ROW, dtype=jnp.int32)[:, None]
    col_of = (jnp.arange(N_COL * EDGES, dtype=jnp.int32) // EDGES)[None, :]
    for level_index in range(LEVELS):
        if level_index == 0:
            update = jnp.zeros((N_ROW, row_span, R, B), jnp.float32)
        else:
            history = jnp.concatenate(levels_done, axis=1)
            sources = edge_sources[level_index - 1]
            usable = sources >= 0
            clipped = jnp.clip(sources, 0, level_index * row_span - 1).astype(jnp.int32)
            picked = history[row_ids, clipped] * usable.astype(jnp.float32)[:, :, None, None]
            terms = jnp.einsum("qerb,qebd->qerd", picked, coupling_blocks[level_index - 1], precision=lax.Precision.HIGHEST)
            targets = edge_targets[level_index - 1]
            flat_target = (targets // DSLOT) * row_span + col_of * DSLOT + targets % DSLOT
            flat_target = jnp.where(usable, flat_target, 0).astype(jnp.int32)
            update = jnp.zeros((N_ROW * row_span, R, B), jnp.float32)
            update = update.at[flat_target.reshape(-1)].add(terms.reshape(-1, R, B))
            update = update.reshape(N_ROW, row_span, R, B)
        alive_mask = jnp.arange(DSLOT, dtype=jnp.int32)[None, None, :] < slot_counts[level_index][:, :, None]
        alive_mask = alive_mask.reshape(N_ROW, row_span)
        solved = jnp.einsum("qsrb,qsbd->qsrd", right_sides[level_index] - update, inverse_blocks[level_index], precision=lax.Precision.HIGHEST)
        solved = jnp.where(alive_mask[:, :, None, None], solved, jnp.float32(0.0))
        levels_done.append(solved)
    return jnp.stack(levels_done)
```

```python
import functools

import jax
import jax.numpy as jnp
from jax import lax
from jax.experimental import pallas as pl
from jax.experimental.pallas import tpu as pltpu
from jax.sharding import PartitionSpec as P

HIGHEST = lax.Precision.HIGHEST
ANY = pl.BlockSpec(memory_space=pl.ANY)
VMEM = pl.BlockSpec(memory_space=pltpu.VMEM)
SMEM = pl.BlockSpec(memory_space=pltpu.SMEM)
LIMIT = 32 * 1024 * 1024
GROUP = 4


def dot(a, b):
    return lax.dot_general(
        a, b, (((1,), (0,)), ((), ())), precision=HIGHEST, preferred_element_type=jnp.float32
    )


def solve_kernel(level, peers, *refs):
    if peers:
        received, counts, right, inverse, solved, copies = refs
    else:
        counts, right, inverse, solved, copies = refs
    for s in range(right.shape[0]):
        value = right[s]
        if peers:
            update = received[s]
            for peer in range(1, peers):
                update = update + received[peer * right.shape[0] + s]
            value = value - update
        value = dot(value, inverse[s])
        value = jnp.where(s < counts[level], value, jnp.zeros_like(value))
        solved[s] = value
        if copies is not None:
            for copy in range(copies.shape[0]):
                copies[copy, s] = value


def last_kernel(level, peers, received, counts, right, inverse, solved):
    solve_kernel(level, peers, received, counts, right, inverse, solved, None)


def solve(level, received, counts, right, inverse):
    block = jax.ShapeDtypeStruct(right.shape, jnp.float32)
    args = (counts, right, inverse)
    specs = [SMEM, VMEM, VMEM]
    peers = 0
    if received is not None:
        peers = received.shape[0] // right.shape[0]
        args, specs = (received,) + args, [VMEM] + specs
    params = pltpu.CompilerParams(vmem_limit_bytes=LIMIT)
    if level == 3:
        return pl.pallas_call(
            functools.partial(last_kernel, level, peers),
            out_shape=block, in_specs=specs, out_specs=VMEM, compiler_params=params,
        )(*args), None
    return pl.pallas_call(
        functools.partial(solve_kernel, level, peers),
        out_shape=(block, jax.ShapeDtypeStruct((GROUP,) + right.shape, jnp.float32)),
        in_specs=specs, out_specs=(VMEM, VMEM), compiler_params=params,
    )(*args)


def edge_kernel(level, edges, parts, *refs):
    part, place, target, coupling = refs[:4]
    history = refs[4 : 4 + parts]
    out, picked, blocks, picked_sem, block_sem = refs[4 + parts :]
    for e in range(edges):
        pltpu.make_async_copy(coupling.at[level - 1, 0, e], blocks.at[e], block_sem.at[e]).start()
    for e in range(edges):
        for index in range(parts):
            @pl.when(part[level - 1, e] == index)
            def _():
                pltpu.make_async_copy(
                    history[index].at[place[level - 1, e]], picked.at[e], picked_sem.at[e]
                ).start()
    out[...] = jnp.zeros_like(out)
    for e in range(edges):
        pltpu.make_async_copy(history[0].at[0], picked.at[e], picked_sem.at[e]).wait()
        pltpu.make_async_copy(coupling.at[level - 1, 0, e], blocks.at[e], block_sem.at[e]).wait()
        goal = target[level - 1, e]
        live = (goal >= 0).astype(jnp.float32)
        goal = jnp.maximum(goal, 0)
        out[goal] = out[goal] + dot(picked[e] * live, blocks[e])


def edge_terms(level, part, place, target, coupling, history, target_total):
    edges = coupling.shape[2]
    rows, order = history[0].shape[1:]
    return pl.pallas_call(
        functools.partial(edge_kernel, level, edges, len(history)),
        out_shape=jax.ShapeDtypeStruct((target_total, rows, order), jnp.float32),
        in_specs=[SMEM, SMEM, SMEM, ANY] + [ANY] * len(history),
        out_specs=VMEM,
        scratch_shapes=[
            pltpu.VMEM((edges, rows, order), jnp.float32),
            pltpu.VMEM((edges, order, order), jnp.float32),
            pltpu.SemaphoreType.DMA((edges,)),
            pltpu.SemaphoreType.DMA((edges,)),
        ],
        compiler_params=pltpu.CompilerParams(vmem_limit_bytes=LIMIT),
    )(part, place, target, coupling, *history)


def gather_col(copies, cols):
    chips = cols // 2
    far = [
        [2 * (GROUP * hi + lo) + core for hi in range(chips // GROUP)]
        for lo in range(GROUP)
        for core in range(2)
    ]

    def shift(x, k):
        return lax.ppermute(x, "col", [(i, (i + 2 * k) % cols) for i in range(cols)])

    mine = lax.all_to_all(copies, "col", 0, 0, tiled=True, axis_index_groups=far)
    half = mine.shape[0] // 2
    below, above = shift(mine, 1), shift(mine, -1)
    low, high = shift(mine[:half], 2), shift(mine[half:], -2)
    same = jnp.concatenate([mine, below, low, high, above])
    return same.reshape((-1,) + same.shape[2:])


def on_device(
    right_sides, inverse_blocks, coupling_blocks, slot_counts, edge_sources, edge_targets
):
    level_total = right_sides.shape[0]
    slots = right_sides.shape[2]
    rows, cols = lax.axis_size("row"), lax.axis_size("col")
    column = lax.axis_index("col")
    core, low_chip = column % 2, (column // 2) % GROUP
    sources = jnp.maximum(edge_sources[:, 0], 0)
    source_level, source_slot = sources // (cols * slots), sources % slots
    source_col = (sources // slots) % cols
    source_chip = source_col // 2
    distance = (low_chip - source_chip) % GROUP
    part = source_level * 2 + (source_col % 2 != core).astype(jnp.int32)
    place = (distance * (cols // 2 // GROUP) + source_chip // GROUP) * slots + source_slot
    targets = edge_targets[:, 0]
    counts = slot_counts[:, 0, 0]
    history, results, received = [], [], None
    for level in range(level_total):
        if level:
            terms = edge_terms(
                level, part, place, targets, coupling_blocks, history, rows * slots
            )
            received = lax.all_to_all(terms, "row", 0, 0, tiled=True)
        solved, copies = solve(
            level, received, counts, right_sides[level, 0], inverse_blocks[level, 0]
        )
        results.append(solved)
        if level + 1 < level_total:
            same = gather_col(copies, cols)
            other = lax.ppermute(same, "col", [(i, i ^ 1) for i in range(cols)])
            history += [same, other]
    return jnp.stack(results)[:, None]


def solution(mesh):
    return jax.shard_map(
        on_device,
        mesh=mesh,
        in_specs=(
            P(None, "row", "col", None, None),
            P(None, "row", "col", None, None),
            P(None, "row", "col", None, None),
            P(None, "row", "col"),
            P(None, "row", "col"),
            P(None, "row", "col"),
        ),
        out_specs=P(None, "row", "col", None, None),
        check_vma=False,
    )
```

```python
import functools

import jax
import jax.numpy as jnp
from jax import lax
from jax.experimental import pallas as pl
from jax.experimental.pallas import tpu as pltpu
from jax.sharding import PartitionSpec as P

HIGHEST = lax.Precision.HIGHEST
ANY = pl.BlockSpec(memory_space=pl.ANY)
VMEM = pl.BlockSpec(memory_space=pltpu.VMEM)
SMEM = pl.BlockSpec(memory_space=pltpu.SMEM)
PARAMS = pltpu.CompilerParams(vmem_limit_bytes=32 * 1024 * 1024)
CORES = 2
STRIDE = 2


def dot(a, b):
    return lax.dot_general(
        a, b, (((1,), (0,)), ((), ())), precision=HIGHEST, preferred_element_type=jnp.float32
    )


def solve_kernel(level, peers, last, *refs):
    received = None
    if peers:
        received, refs = refs[0], refs[1:]
    counts, right_all, inverse_all = refs[:3]
    earlier = refs[3 : 3 + level] if last else ()
    outs = refs[3 + len(earlier) : -3]
    right, inverse, sem = refs[-3:]
    loads = [
        pltpu.make_async_copy(right_all.at[level, 0], right, sem.at[0]),
        pltpu.make_async_copy(inverse_all.at[level, 0], inverse, sem.at[1]),
    ]
    for load in loads:
        load.start()
    slots = right.shape[0]
    updates = []
    if peers:
        for s in range(slots):
            update = received[s]
            for peer in range(1, peers):
                update = update + received[peer * slots + s]
            updates.append(update)
    if last:
        for index, block in enumerate(earlier):
            outs[0][index, 0] = block[...]
    for load in loads:
        load.wait()
    for s in range(slots):
        value = right[s]
        if peers:
            value = value - updates[s]
        value = dot(value, inverse[s])
        value = jnp.where(s < counts[level, 0, 0], value, jnp.zeros_like(value))
        if last:
            outs[0][level, 0, s] = value
        else:
            outs[0][s] = value
            for copy in range(outs[1].shape[0]):
                outs[1][copy, s] = value


def solve(level, received, counts, right, inverse, earlier, fan):
    slots, rows, order = right.shape[2:]
    last = level + 1 == right.shape[0]
    args, specs, peers = (counts, right, inverse), [SMEM, ANY, ANY], 0
    if received is not None:
        peers = received.shape[0] // slots
        args, specs = (received,) + args, [VMEM] + specs
    if last:
        args, specs = args + tuple(earlier), specs + [VMEM] * len(earlier)
        shapes, outs = jax.ShapeDtypeStruct(right.shape, jnp.float32), VMEM
    else:
        shapes = (
            jax.ShapeDtypeStruct((slots, rows, order), jnp.float32),
            jax.ShapeDtypeStruct((fan, slots, rows, order), jnp.float32),
        )
        outs = (VMEM, VMEM)
    return pl.pallas_call(
        functools.partial(solve_kernel, level, peers, last),
        out_shape=shapes, in_specs=specs, out_specs=outs,
        scratch_shapes=[
            pltpu.VMEM((slots, rows, order), jnp.float32),
            pltpu.VMEM((slots, order, order), jnp.float32),
            pltpu.SemaphoreType.DMA((2,)),
        ],
        compiler_params=PARAMS,
    )(*args)


def edge_kernel(level, edges, cols, slots, column, source, target, coupling, *refs):
    parts = level * CORES
    history = refs[:parts]
    out, picked, blocks, products, picked_sem, block_sem = refs[parts:]
    block_copy = pltpu.make_async_copy(coupling.at[level - 1, 0], blocks, block_sem)
    block_copy.start()
    core, chip = column[0] % CORES, column[0] // CORES
    chips = cols // CORES
    for e in range(edges):
        p = jnp.maximum(source[level - 1, 0, e], 0)
        where = (p // slots) % cols
        there = where // CORES
        part = (p // (slots * cols)) * CORES + ((where % CORES) != core).astype(jnp.int32)
        group = (there % STRIDE - chip % STRIDE) % STRIDE
        place = (group * (chips // STRIDE) + there // STRIDE) * slots + p % slots
        for index in range(parts):
            @pl.when(part == index)
            def _():
                pltpu.make_async_copy(
                    history[index].at[place], picked.at[e], picked_sem.at[e]
                ).start()
    out[...] = jnp.zeros_like(out)
    for e in range(edges):
        pltpu.make_async_copy(history[0].at[0], picked.at[e], picked_sem.at[e]).wait()
    block_copy.wait()
    for e in range(edges):
        products[e] = dot(picked[e], blocks[e])
    for e in range(edges):
        goal = target[level - 1, 0, e]
        live = (goal >= 0).astype(jnp.float32)
        goal = jnp.maximum(goal, 0)
        out[goal] = out[goal] + products[e] * live


def edge_terms(level, column, source, target, coupling, history, target_total, cols, slots):
    edges = coupling.shape[2]
    rows, order = history[0].shape[1:]
    return pl.pallas_call(
        functools.partial(edge_kernel, level, edges, cols, slots),
        out_shape=jax.ShapeDtypeStruct((target_total, rows, order), jnp.float32),
        in_specs=[SMEM, SMEM, SMEM, ANY] + [ANY] * len(history),
        out_specs=VMEM,
        scratch_shapes=[
            pltpu.VMEM((edges, rows, order), jnp.float32),
            pltpu.VMEM((edges, order, order), jnp.float32),
            pltpu.VMEM((edges, rows, order), jnp.float32),
            pltpu.SemaphoreType.DMA((edges,)),
            pltpu.SemaphoreType.DMA,
        ],
        compiler_params=PARAMS,
    )(column, source, target, coupling, *history)


def gather_col(copies, cols):
    chips = cols // CORES
    far = [
        [CORES * (STRIDE * hi + lo) + core for hi in range(chips // STRIDE)]
        for lo in range(STRIDE)
        for core in range(CORES)
    ]

    def shift(x, k):
        return lax.ppermute(x, "col", [(i, (i + CORES * k) % cols) for i in range(cols)])

    mine = lax.all_to_all(copies, "col", 0, 0, tiled=True, axis_index_groups=far)
    half = mine.shape[0] // 2
    same = jnp.concatenate([mine, shift(mine[:half], 1), shift(mine[half:], -1)])
    return same.reshape((-1,) + same.shape[2:])


def on_device(
    right_sides, inverse_blocks, coupling_blocks, slot_counts, edge_sources, edge_targets
):
    level_total = right_sides.shape[0]
    slots = right_sides.shape[2]
    rows, cols = lax.axis_size("row"), lax.axis_size("col")
    column = lax.axis_index("col").reshape(1).astype(jnp.int32)
    history, results, received = [], [], None
    for level in range(level_total):
        if level:
            terms = edge_terms(
                level, column, edge_sources, edge_targets, coupling_blocks, history,
                rows * slots, cols, slots,
            )
            received = lax.all_to_all(terms, "row", 0, 0, tiled=True)
        solved = solve(
            level, received, slot_counts, right_sides, inverse_blocks, results,
            cols // CORES // STRIDE,
        )
        if level + 1 == level_total:
            return solved
        results.append(solved[0])
        same = gather_col(solved[1], cols)
        other = lax.ppermute(same, "col", [(i, i ^ 1) for i in range(cols)])
        history += [same, other]


def solution(mesh):
    return jax.shard_map(
        on_device,
        mesh=mesh,
        in_specs=(
            P(None, "row", "col", None, None),
            P(None, "row", "col", None, None),
            P(None, "row", "col", None, None),
            P(None, "row", "col"),
            P(None, "row", "col"),
            P(None, "row", "col"),
        ),
        out_specs=P(None, "row", "col", None, None),
        check_vma=False,
    )
```

```python
import functools

import jax
import jax.numpy as jnp
from jax import lax
from jax.experimental import pallas as pl
from jax.experimental.pallas import tpu as pltpu
from jax.sharding import PartitionSpec as P

HIGHEST = lax.Precision.HIGHEST
ANY = pl.BlockSpec(memory_space=pl.ANY)
HBM = pl.BlockSpec(memory_space=pltpu.HBM)
VMEM = pl.BlockSpec(memory_space=pltpu.VMEM)
SMEM = pl.BlockSpec(memory_space=pltpu.SMEM)
PARAMS = pltpu.CompilerParams(vmem_limit_bytes=32 * 1024 * 1024)
CORES = 2
STRIDE = 4


def dot(a, b):
    return lax.dot_general(
        a, b, (((1,), (0,)), ((), ())), precision=HIGHEST, preferred_element_type=jnp.float32
    )


def solve_kernel(level, peers, last, *refs):
    received = None
    if peers:
        received, refs = refs[0], refs[1:]
    counts, right_all, inverse_all = refs[:3]
    earlier = refs[3 : 3 + level] if last else ()
    outs = refs[3 + len(earlier) : -3]
    right, inverse, sem = refs[-3:]
    loads = [
        pltpu.make_async_copy(right_all.at[level, 0], right, sem.at[0]),
        pltpu.make_async_copy(inverse_all.at[level, 0], inverse, sem.at[1]),
    ]
    for load in loads:
        load.start()
    slots = right.shape[0]
    updates = []
    if peers:
        for s in range(slots):
            update = received[s]
            for peer in range(1, peers):
                update = update + received[peer * slots + s]
            updates.append(update)
    if last:
        for index, block in enumerate(earlier):
            outs[0][index, 0] = block[...]
    for load in loads:
        load.wait()
    for s in range(slots):
        value = right[s]
        if peers:
            value = value - updates[s]
        value = dot(value, inverse[s])
        value = jnp.where(s < counts[0, 0, level], value, jnp.zeros_like(value))
        if last:
            outs[0][level, 0, s] = value
        else:
            outs[0][s] = value


def solve(level, received, counts, right, inverse, earlier):
    slots, rows, order = right.shape[2:]
    last = level + 1 == right.shape[0]
    args, specs, peers = (counts, right, inverse), [SMEM, HBM, HBM], 0
    if received is not None:
        peers = received.shape[0] // slots
        args, specs = (received,) + args, [VMEM] + specs
    if last:
        args, specs = args + tuple(earlier), specs + [VMEM] * len(earlier)
        shapes, outs = jax.ShapeDtypeStruct(right.shape, jnp.float32), VMEM
    else:
        shapes, outs = jax.ShapeDtypeStruct((slots, rows, order), jnp.float32), VMEM
    return pl.pallas_call(
        functools.partial(solve_kernel, level, peers, last),
        out_shape=shapes, in_specs=specs, out_specs=outs,
        scratch_shapes=[
            pltpu.VMEM((slots, rows, order), jnp.float32),
            pltpu.VMEM((slots, order, order), jnp.float32),
            pltpu.SemaphoreType.DMA((2,)),
        ],
        compiler_params=PARAMS,
    )(*args)


def edge_kernel(level, edges, cols, slots, column, source, target, coupling, *refs):
    parts = level * CORES
    history = refs[:parts]
    out, picked, blocks, products, picked_sem, block_sem = refs[parts:]
    block_copy = pltpu.make_async_copy(coupling.at[level - 1, 0], blocks, block_sem)
    block_copy.start()
    core, chip = column[0] % CORES, column[0] // CORES
    chips = cols // CORES
    for e in range(edges):
        p = jnp.maximum(source[level - 1, 0, e], 0)
        where = (p // slots) % cols
        there = where // CORES
        part = (p // (slots * cols)) * CORES + ((where % CORES) != core).astype(jnp.int32)
        group = (chip + STRIDE - there % STRIDE) % STRIDE
        place = (group * (chips // STRIDE) + there // STRIDE) * slots + p % slots
        for index in range(parts):
            @pl.when(part == index)
            def _():
                pltpu.make_async_copy(
                    history[index].at[place], picked.at[e], picked_sem.at[e]
                ).start()
    out[...] = jnp.zeros_like(out)
    for e in range(edges):
        pltpu.make_async_copy(history[0].at[0], picked.at[e], picked_sem.at[e]).wait()
    block_copy.wait()
    for e in range(edges):
        products[e] = dot(picked[e], blocks[e])
    for e in range(edges):
        goal = target[level - 1, 0, e]
        live = (goal >= 0).astype(jnp.float32)
        goal = jnp.maximum(goal, 0)
        out[goal] = out[goal] + products[e] * live


def edge_terms(level, column, source, target, coupling, history, target_total, cols, slots):
    edges = coupling.shape[2]
    rows, order = history[0].shape[1:]
    return pl.pallas_call(
        functools.partial(edge_kernel, level, edges, cols, slots),
        out_shape=jax.ShapeDtypeStruct((target_total, rows, order), jnp.float32),
        in_specs=[SMEM, SMEM, SMEM, ANY] + [ANY] * len(history),
        out_specs=VMEM,
        scratch_shapes=[
            pltpu.VMEM((edges, rows, order), jnp.float32),
            pltpu.VMEM((edges, order, order), jnp.float32),
            pltpu.VMEM((edges, rows, order), jnp.float32),
            pltpu.SemaphoreType.DMA((edges,)),
            pltpu.SemaphoreType.DMA,
        ],
        compiler_params=PARAMS,
    )(column, source, target, coupling, *history)


def gather_col(solved, cols):
    chips = cols // CORES
    far = [
        [CORES * (STRIDE * hi + lo) + core for hi in range(chips // STRIDE)]
        for lo in range(STRIDE)
        for core in range(CORES)
    ]

    def shift(x, k):
        return lax.ppermute(x, "col", [(i, (i + CORES * k) % cols) for i in range(cols)])

    mine = lax.all_gather(solved, "col", axis=0, tiled=False, axis_index_groups=far)
    half = mine.shape[0] // 2
    below, above = shift(mine, 1), shift(mine, -1)
    low, high = shift(mine[:half], 2), shift(mine[half:], -2)
    same = jnp.concatenate([mine, below, low, high, above])
    return same.reshape((-1,) + same.shape[2:])


def on_device(
    right_sides, inverse_blocks, coupling_blocks, slot_counts, edge_sources, edge_targets
):
    level_total = right_sides.shape[0]
    slots = right_sides.shape[2]
    rows, cols = lax.axis_size("row"), lax.axis_size("col")
    column = lax.axis_index("col").reshape(1).astype(jnp.int32)
    counts = jnp.transpose(slot_counts, (1, 2, 0))
    history, results, received = [], [], None
    for level in range(level_total):
        if level:
            terms = edge_terms(
                level, column, edge_sources, edge_targets, coupling_blocks, history,
                rows * slots, cols, slots,
            )
            received = lax.all_to_all(terms, "row", 0, 0, tiled=True)
        solved = solve(
            level, received, counts, right_sides, inverse_blocks, results,
        )
        if level + 1 == level_total:
            return solved
        results.append(solved)
        same = gather_col(solved, cols)
        other = lax.ppermute(same, "col", [(i, i ^ 1) for i in range(cols)])
        history += [same, other]


def solution(mesh):
    return jax.shard_map(
        on_device,
        mesh=mesh,
        in_specs=(
            P(None, "row", "col", None, None),
            P(None, "row", "col", None, None),
            P(None, "row", "col", None, None),
            P(None, "row", "col"),
            P(None, "row", "col"),
            P(None, "row", "col"),
        ),
        out_specs=P(None, "row", "col", None, None),
        check_vma=False,
    )
```

```python
import functools

import jax
import jax.numpy as jnp
from jax import lax
from jax.experimental import pallas as pl
from jax.experimental.pallas import tpu as pltpu
from jax.sharding import PartitionSpec as P

HIGHEST = lax.Precision.HIGHEST
ANY = pl.BlockSpec(memory_space=pl.ANY)
VMEM = pl.BlockSpec(memory_space=pltpu.VMEM)
SMEM = pl.BlockSpec(memory_space=pltpu.SMEM)
PARAMS = pltpu.CompilerParams(vmem_limit_bytes=32 * 1024 * 1024)
CORES = 2
STRIDE = 4


def dot(a, b):
    return lax.dot_general(
        a, b, (((1,), (0,)), ((), ())), precision=HIGHEST, preferred_element_type=jnp.float32
    )


def half_kernel(level, peers, levels, *refs):
    received = None
    if peers:
        received, refs = refs[0], refs[1:]
    core = refs[0][0] % CORES
    infos, rights, inverses = refs[1:3], refs[3:5], refs[5:7]
    out, right, inverse, sem = refs[7:]
    slots, half = right.shape[1:3]
    first = pl.multiple_of(core * half, half)
    loads = []
    for c in range(CORES):
        loads.append(pltpu.make_async_copy(
            rights[c].at[level, 0, :, pl.ds(first, half)], right.at[c], sem.at[2 * c]))
        loads.append(pltpu.make_async_copy(
            inverses[c].at[level, 0], inverse.at[c], sem.at[2 * c + 1]))
    for load in loads:
        load.start()
    updates = []
    if peers:
        for s in range(CORES * slots):
            update = received[s]
            for peer in range(1, peers):
                update = update + received[peer * CORES * slots + s]
            updates.append(update)
    for load in loads:
        load.wait()
    for c in range(CORES):
        for s in range(slots):
            value = right[c, s]
            if peers:
                value = value - updates[c * slots + s]
            value = dot(value, inverse[c, s])
            live = s < infos[c][2 * (levels - 1) + level, 0]
            out[c * slots + s] = jnp.where(live, value, jnp.zeros_like(value))


def half_solve(level, received, column, infos, rights, inverses):
    levels, _, slots, rows, order = rights[0].shape
    half = rows // CORES
    args, specs, peers = (), [], 0
    if received is not None:
        peers = received.shape[0] // (CORES * slots)
        args, specs = (received,), [VMEM]
    return pl.pallas_call(
        functools.partial(half_kernel, level, peers, levels),
        out_shape=jax.ShapeDtypeStruct((CORES * slots, half, order), jnp.float32),
        in_specs=specs + [SMEM] * 3 + [ANY] * 4,
        out_specs=VMEM,
        scratch_shapes=[
            pltpu.VMEM((CORES, slots, half, order), jnp.float32),
            pltpu.VMEM((CORES, slots, order, order), jnp.float32),
            pltpu.SemaphoreType.DMA((2 * CORES,)),
        ],
        compiler_params=PARAMS,
    )(*args, column, *infos, *rights, *inverses)


def last_kernel(level, peers, *refs):
    received, column, info, right_all, inverse_all = refs[:5]
    mine, theirs = refs[5 : 5 + level], refs[5 + level]
    out, right, inverse, sem = refs[6 + level :]
    slots, rows = right.shape[:2]
    half = rows // CORES
    core = column[0] % CORES
    loads = [
        pltpu.make_async_copy(right_all.at[level, 0], right, sem.at[0]),
        pltpu.make_async_copy(inverse_all.at[level, 0], inverse, sem.at[1]),
    ]
    for load in loads:
        load.start()
    near = pl.multiple_of(core * half, half)
    away = pl.multiple_of((1 - core) * half, half)
    for index in range(level):
        for s in range(slots):
            out[index, 0, s, pl.ds(near, half), :] = mine[index][s]
            out[index, 0, s, pl.ds(away, half), :] = theirs[index, s]
    updates = []
    for s in range(slots):
        pieces = []
        for c in range(CORES):
            update = received[c * slots + s]
            for peer in range(1, peers):
                update = update + received[(peer * CORES + c) * slots + s]
            pieces.append(update)
        updates.append(jnp.concatenate(pieces, axis=0))
    for load in loads:
        load.wait()
    for s in range(slots):
        value = dot(right[s] - updates[s], inverse[s])
        live = s < info[2 * level + level, 0]
        out[level, 0, s] = jnp.where(live, value, jnp.zeros_like(value))


def last_solve(received, column, info, right, inverse, mine, theirs):
    levels, _, slots, rows, order = right.shape
    return pl.pallas_call(
        functools.partial(last_kernel, levels - 1, received.shape[0] // (CORES * slots)),
        out_shape=jax.ShapeDtypeStruct(right.shape, jnp.float32),
        in_specs=[VMEM, SMEM, SMEM, ANY, ANY] + [VMEM] * (len(mine) + 1),
        out_specs=VMEM,
        scratch_shapes=[
            pltpu.VMEM((slots, rows, order), jnp.float32),
            pltpu.VMEM((slots, order, order), jnp.float32),
            pltpu.SemaphoreType.DMA((2,)),
        ],
        compiler_params=PARAMS,
    )(received, column, info, right, inverse, *mine, theirs)


def edge_kernel(level, last, edges, cols, slots, column, *refs):
    infos, couplings, history = refs[:2], refs[2:4], refs[4 : 4 + level]
    out, picked, blocks, products, picked_sem, block_sem = refs[4 + level :]
    block_copies = [
        pltpu.make_async_copy(couplings[c].at[level - 1, 0], blocks.at[c], block_sem.at[c])
        for c in range(CORES)
    ]
    for copy in block_copies:
        copy.start()
    core, chip = column[0] % CORES, column[0] // CORES
    levels_after = infos[0].shape[0]
    target_row = (levels_after - 1) // 3
    chips = cols // CORES
    for c in range(CORES):
        for e in range(edges):
            p = jnp.maximum(infos[c][level - 1, e], 0)
            where = (p // slots) % cols
            there = where // CORES
            other = ((where % CORES) != core).astype(jnp.int32)
            group = (chip + STRIDE - there % STRIDE) % STRIDE
            place = ((group * (chips // STRIDE) + there // STRIDE) * CORES + other) * slots
            place = place + p % slots
            for index in range(level):
                @pl.when(p // (slots * cols) == index)
                def _():
                    pltpu.make_async_copy(
                        history[index].at[place], picked.at[c, e], picked_sem.at[c, e]
                    ).start()
    out[...] = jnp.zeros_like(out)
    for c in range(CORES):
        for e in range(edges):
            pltpu.make_async_copy(
                history[0].at[0], picked.at[c, e], picked_sem.at[c, e]
            ).wait()
        block_copies[c].wait()
    for c in range(CORES):
        for e in range(edges):
            products[c, e] = dot(picked[c, e], blocks[c, e])
    for c in range(CORES):
        slot_of = jnp.where(core == c, 0, 1) if last else c
        for e in range(edges):
            goal = infos[c][target_row + level - 1, e]
            live = (goal >= 0).astype(jnp.float32)
            goal = jnp.maximum(goal, 0)
            goal = ((goal // slots) * CORES + slot_of) * slots + goal % slots
            out[goal] = out[goal] + products[c, e] * live


def edge_terms(level, last, column, infos, couplings, history, row_total, cols, slots):
    edges = couplings[0].shape[2]
    rows, order = history[0].shape[1:]
    return pl.pallas_call(
        functools.partial(edge_kernel, level, last, edges, cols, slots),
        out_shape=jax.ShapeDtypeStruct((row_total * CORES * slots, rows, order), jnp.float32),
        in_specs=[SMEM] * 3 + [ANY] * (2 + len(history)),
        out_specs=VMEM,
        scratch_shapes=[
            pltpu.VMEM((CORES, edges, rows, order), jnp.float32),
            pltpu.VMEM((CORES, edges, order, order), jnp.float32),
            pltpu.VMEM((CORES, edges, rows, order), jnp.float32),
            pltpu.SemaphoreType.DMA((CORES, edges)),
            pltpu.SemaphoreType.DMA((CORES,)),
        ],
        compiler_params=PARAMS,
    )(column, *infos, *couplings, *history)


def swap(x, cols):
    return lax.ppermute(x, "col", [(i, i ^ 1) for i in range(cols)])


def gather_far(solved, cols):
    far = [
        [CORES * (STRIDE * hi + lo) + core for hi in range(cols // CORES // STRIDE)]
        for lo in range(STRIDE)
        for core in range(CORES)
    ]
    return lax.all_gather(solved, "col", axis=0, tiled=False, axis_index_groups=far)


def gather_near(mine, cols):
    def shift(x, k):
        return lax.ppermute(x, "col", [(i, (i + CORES * k) % cols) for i in range(cols)])

    half = mine.shape[0] // 2
    below, above = shift(mine, 1), shift(mine, -1)
    low, high = shift(mine[:half], 2), shift(mine[half:], -2)
    same = jnp.concatenate([mine, below, low, high, above])
    return same.reshape((-1,) + same.shape[2:])


def on_device(
    right_sides, inverse_blocks, coupling_blocks, slot_counts, edge_sources, edge_targets
):
    level_total, _, slots = right_sides.shape[:3]
    edges = edge_sources.shape[2]
    rows, cols = lax.axis_size("row"), lax.axis_size("col")
    column = lax.axis_index("col").reshape(1).astype(jnp.int32)
    info = jnp.concatenate([
        edge_sources[:, 0],
        edge_targets[:, 0],
        jnp.broadcast_to(slot_counts[:, 0], (level_total, edges)),
    ])
    rights = (right_sides, swap(right_sides, cols))
    inverses = (inverse_blocks, swap(inverse_blocks, cols))
    infos = (info, swap(info, cols))
    history, results, received = [], [], None
    for level in range(level_total - 1):
        if level:
            terms = edge_terms(
                level, False, column, infos, couplings, history, rows, cols, slots
            )
            received = lax.all_to_all(terms, "row", 0, 0, tiled=True)
        solved = half_solve(level, received, column, infos, rights, inverses)
        results.append(solved)
        mine = gather_far(solved, cols)
        if level == 0:
            coupling, mine = lax.optimization_barrier((coupling_blocks, mine))
            couplings = (coupling_blocks, swap(coupling, cols))
        history.append(gather_near(mine, cols))
    terms = edge_terms(
        level_total - 1, True, column, infos, couplings, history, rows, cols, slots
    )
    theirs = swap(jnp.stack([block[slots:] for block in results]), cols)
    chip_groups = [
        [row * cols + CORES * chip + core for row in range(rows) for core in range(CORES)]
        for chip in range(cols // CORES)
    ]
    received = lax.all_to_all(
        terms, ("row", "col"), 0, 0, tiled=True, axis_index_groups=chip_groups
    )
    return last_solve(
        received, column, info, right_sides, inverse_blocks, results, theirs
    )


def solution(mesh):
    return jax.shard_map(
        on_device,
        mesh=mesh,
        in_specs=(
            P(None, "row", "col", None, None),
            P(None, "row", "col", None, None),
            P(None, "row", "col", None, None),
            P(None, "row", "col"),
            P(None, "row", "col"),
            P(None, "row", "col"),
        ),
        out_specs=P(None, "row", "col", None, None),
        check_vma=False,
    )
```

```python
import functools

import jax
import jax.numpy as jnp
from jax import lax
from jax.experimental import pallas as pl
from jax.experimental.pallas import tpu as pltpu
from jax.sharding import PartitionSpec as P

HIGHEST = lax.Precision.HIGHEST
ANY = pl.BlockSpec(memory_space=pl.ANY)
VMEM = pl.BlockSpec(memory_space=pltpu.VMEM)
SMEM = pl.BlockSpec(memory_space=pltpu.SMEM)
PARAMS = pltpu.CompilerParams(vmem_limit_bytes=32 * 1024 * 1024)
CORES = 2
STRIDE = 4


def dot(a, b):
    return lax.dot_general(
        a, b, (((1,), (0,)), ((), ())), precision=HIGHEST, preferred_element_type=jnp.float32
    )


def first_kernel(counts, right_all, inverse_all, out, right, inverse, sem):
    loads = [
        pltpu.make_async_copy(right_all.at[0, 0], right, sem.at[0]),
        pltpu.make_async_copy(inverse_all.at[0, 0], inverse, sem.at[1]),
    ]
    for load in loads:
        load.start()
    for load in loads:
        load.wait()
    for s in range(right.shape[0]):
        value = dot(right[s], inverse[s])
        out[s] = jnp.where(s < counts[0, 0, 0], value, jnp.zeros_like(value))


def first_solve(counts, right, inverse):
    slots, rows, order = right.shape[2:]
    return pl.pallas_call(
        first_kernel,
        out_shape=jax.ShapeDtypeStruct((slots, rows, order), jnp.float32),
        in_specs=[SMEM, ANY, ANY],
        out_specs=VMEM,
        scratch_shapes=[
            pltpu.VMEM((slots, rows, order), jnp.float32),
            pltpu.VMEM((slots, order, order), jnp.float32),
            pltpu.SemaphoreType.DMA((2,)),
        ],
        compiler_params=pltpu.CompilerParams(vmem_limit_bytes=60 * 1024 * 1024),
    )(counts, right, inverse)


def solve_kernel(level, last, received, counts, right, inverse, *refs):
    earlier, out = refs[:-1], refs[-1]
    slots = right.shape[2]
    peers = received.shape[0] // (CORES * slots)
    for index, block in enumerate(earlier):
        out[index, 0] = block[...]
    for s in range(slots):
        pieces = []
        for c in range(CORES):
            update = received[c * slots + s]
            for peer in range(1, peers):
                update = update + received[(peer * CORES + c) * slots + s]
            pieces.append(update)
        update = jnp.concatenate(pieces, axis=0)
        value = dot(right[level, 0, s] - update, inverse[level, 0, s])
        value = jnp.where(s < counts[0, 0, level], value, jnp.zeros_like(value))
        if last:
            out[level, 0, s] = value
        else:
            out[s] = value


def solve(level, received, counts, right, inverse, results):
    last = level + 1 == right.shape[0]
    earlier = results if last else []
    shape = right.shape if last else right.shape[2:]
    return pl.pallas_call(
        functools.partial(solve_kernel, level, last),
        out_shape=jax.ShapeDtypeStruct(shape, jnp.float32),
        in_specs=[VMEM, SMEM, VMEM, VMEM] + [VMEM] * len(earlier),
        out_specs=VMEM,
        compiler_params=PARAMS,
    )(received, counts, right, inverse, *earlier)


def edge_kernel(level, edges, cols, slots, column, *refs):
    infos, couplings, history = refs[:2], refs[2:4], refs[4 : 4 + level]
    out, products = refs[4 + level :]
    core, chip = column[0] % CORES, column[0] // CORES
    chips = cols // CORES
    target_row = infos[0].shape[0] // 2
    for c in range(CORES):
        for e in range(edges):
            p = jnp.maximum(infos[c][level - 1, e], 0)
            where = (p // slots) % cols
            there = where // CORES
            other = ((where % CORES) != core).astype(jnp.int32)
            group = (chip + STRIDE - there % STRIDE) % STRIDE
            place = ((group * (chips // STRIDE) + there // STRIDE) * CORES + other) * slots
            place = place + p % slots
            source_level = p // (slots * cols)
            block = history[0][place]
            for index in range(1, level):
                block = jnp.where(source_level == index, history[index][place], block)
            products[c, e] = dot(block, couplings[c][level - 1, 0, e])
    out[...] = jnp.zeros_like(out)
    for c in range(CORES):
        owner = jnp.where(core == c, 0, 1)
        for e in range(edges):
            goal = infos[c][target_row + level - 1, e]
            live = (goal >= 0).astype(jnp.float32)
            goal = jnp.maximum(goal, 0)
            goal = ((goal // slots) * CORES + owner) * slots + goal % slots
            out[goal] = out[goal] + products[c, e] * live


def edge_terms(level, column, infos, couplings, history, row_total, cols, slots):
    edges = couplings[0].shape[2]
    rows, order = history[0].shape[1:]
    return pl.pallas_call(
        functools.partial(edge_kernel, level, edges, cols, slots),
        out_shape=jax.ShapeDtypeStruct((row_total * CORES * slots, rows, order), jnp.float32),
        in_specs=[SMEM] * 3 + [VMEM] * (2 + len(history)),
        out_specs=VMEM,
        scratch_shapes=[pltpu.VMEM((CORES, edges, rows, order), jnp.float32)],
        compiler_params=PARAMS,
    )(column, *infos, *couplings, *history)


def swap(x, cols):
    return lax.ppermute(x, "col", [(i, i ^ 1) for i in range(cols)])


def gather_far(solved, cols):
    far = [
        [CORES * (STRIDE * hi + lo) + core for hi in range(cols // CORES // STRIDE)]
        for lo in range(STRIDE)
        for core in range(CORES)
    ]
    return lax.all_gather(solved, "col", axis=0, tiled=False, axis_index_groups=far)


def gather_near(mine, cols):
    def shift(x, k):
        return lax.ppermute(x, "col", [(i, (i + CORES * k) % cols) for i in range(cols)])

    half = mine.shape[0] // 2
    below, above = shift(mine, 1), shift(mine, -1)
    low, high = shift(mine[:half], 2), shift(mine[half:], -2)
    same = jnp.concatenate([mine, below, low, high, above])
    return same.reshape((-1,) + same.shape[2:])


def split_rows(solved, core, cols):
    pairs = [[CORES * chip + core for core in range(CORES)] for chip in range(cols // CORES)]
    both = lax.all_gather(solved, "col", axis=0, tiled=False, axis_index_groups=pairs)
    half = both.shape[2] // CORES
    both = lax.dynamic_slice_in_dim(both, core * half, half, axis=2)
    both = jnp.where(core == 0, both, jnp.flip(both, axis=0))
    return both.reshape((-1,) + both.shape[2:])


def on_device(
    right_sides, inverse_blocks, coupling_blocks, slot_counts, edge_sources, edge_targets
):
    level_total, _, slots = right_sides.shape[:3]
    rows, cols = lax.axis_size("row"), lax.axis_size("col")
    column = lax.axis_index("col").astype(jnp.int32)
    counts = jnp.transpose(slot_counts, (1, 2, 0))
    chip_groups = [
        [row * cols + CORES * chip + core for row in range(rows) for core in range(CORES)]
        for chip in range(cols // CORES)
    ]
    solved = first_solve(counts, right_sides, inverse_blocks)
    history, results = [], []
    for level in range(1, level_total):
        results.append(solved)
        mine = gather_far(split_rows(solved, column % CORES, cols), cols)
        if level == 1:
            coupling, sources, targets, mine = lax.optimization_barrier(
                (coupling_blocks, edge_sources[:, 0], edge_targets[:, 0], mine)
            )
            info = jnp.concatenate([sources, targets])
            infos = (info, swap(info, cols))
            couplings = (coupling_blocks, swap(coupling, cols))
        history.append(gather_near(mine, cols))
        terms = edge_terms(
            level, column.reshape(1), infos, couplings, history, rows, cols, slots
        )
        received = lax.all_to_all(
            terms, ("row", "col"), 0, 0, tiled=True, axis_index_groups=chip_groups
        )
        solved = solve(level, received, counts, right_sides, inverse_blocks, results)
    return solved


def solution(mesh):
    return jax.shard_map(
        on_device,
        mesh=mesh,
        in_specs=(
            P(None, "row", "col", None, None),
            P(None, "row", "col", None, None),
            P(None, "row", "col", None, None),
            P(None, "row", "col"),
            P(None, "row", "col"),
            P(None, "row", "col"),
        ),
        out_specs=P(None, "row", "col", None, None),
        check_vma=False,
    )
```

```python
import functools

import jax
import jax.numpy as jnp
from jax import lax
from jax.experimental import pallas as pl
from jax.experimental.pallas import tpu as pltpu
from jax.sharding import PartitionSpec as P

HIGHEST = lax.Precision.HIGHEST
ANY = pl.BlockSpec(memory_space=pl.ANY)
VMEM = pl.BlockSpec(memory_space=pltpu.VMEM)
SMEM = pl.BlockSpec(memory_space=pltpu.SMEM)
PARAMS = pltpu.CompilerParams(vmem_limit_bytes=32 * 1024 * 1024)
CORES = 2
STRIDE = 4


def dot(a, b):
    return lax.dot_general(
        a, b, (((1,), (0,)), ((), ())), precision=HIGHEST, preferred_element_type=jnp.float32
    )


def first_kernel(counts, right_all, inverse_all, out, right, inverse, sem):
    loads = [
        pltpu.make_async_copy(right_all.at[0, 0], right, sem.at[0]),
        pltpu.make_async_copy(inverse_all.at[0, 0], inverse, sem.at[1]),
    ]
    for load in loads:
        load.start()
    for load in loads:
        load.wait()
    for s in range(right.shape[0]):
        value = dot(right[s], inverse[s])
        out[s] = jnp.where(s < counts[0, 0, 0], value, jnp.zeros_like(value))


def first_solve(counts, right, inverse):
    slots, rows, order = right.shape[2:]
    return pl.pallas_call(
        first_kernel,
        out_shape=jax.ShapeDtypeStruct((slots, rows, order), jnp.float32),
        in_specs=[SMEM, ANY, ANY],
        out_specs=VMEM,
        scratch_shapes=[
            pltpu.VMEM((slots, rows, order), jnp.float32),
            pltpu.VMEM((slots, order, order), jnp.float32),
            pltpu.SemaphoreType.DMA((2,)),
        ],
        compiler_params=pltpu.CompilerParams(vmem_limit_bytes=60 * 1024 * 1024),
    )(counts, right, inverse)


def half_kernel(level, received, column, info, other_info, right, inverse, packed, out):
    levels, _, slots, rows = right.shape[:4]
    half, order = rows // CORES, inverse.shape[3]
    peers = received.shape[0] // (CORES * slots)
    first = pl.multiple_of((column[0] % CORES) * half, half)
    kept = levels - 2
    for c in range(CORES):
        for s in range(slots):
            index = c * slots + s
            update = received[index]
            for peer in range(1, peers):
                update = update + received[peer * CORES * slots + index]
            if c == 0:
                value = right[level, 0, s, pl.ds(first, half), :]
                weight = inverse[level, 0, s]
                count = info[2 * (levels - 1) + level, 0]
            else:
                place = (level - 1) * slots + s
                start = pl.multiple_of(place * rows + first, half)
                value = packed[pl.ds(start, half), :]
                weight = packed[pl.ds(kept * slots * rows + place * order, order), :]
                count = other_info[2 * (levels - 1) + level, 0]
            value = dot(value - update, weight)
            out[index] = jnp.where(s < count, value, jnp.zeros_like(value))


def half_solve(level, received, column, infos, right, inverse, packed):
    slots, rows, order = right.shape[2:]
    return pl.pallas_call(
        functools.partial(half_kernel, level),
        out_shape=jax.ShapeDtypeStruct((CORES * slots, rows // CORES, order), jnp.float32),
        in_specs=[VMEM, SMEM, SMEM, SMEM, VMEM, VMEM, VMEM],
        out_specs=VMEM,
        compiler_params=PARAMS,
    )(received, column, *infos, right, inverse, packed)


def last_kernel(level, received, column, info, right, inverse, first, *refs):
    mine, theirs, out = refs[: level - 1], refs[level - 1], refs[level]
    slots, rows = right.shape[2:4]
    half = rows // CORES
    peers = received.shape[0] // (CORES * slots)
    core = column[0] % CORES
    near = pl.multiple_of(core * half, half)
    away = pl.multiple_of((1 - core) * half, half)
    out[0, 0] = first[...]
    for index in range(1, level):
        for s in range(slots):
            out[index, 0, s, pl.ds(near, half), :] = mine[index - 1][s]
            out[index, 0, s, pl.ds(away, half), :] = theirs[index - 1, s]
    for s in range(slots):
        pieces = []
        for c in range(CORES):
            update = received[c * slots + s]
            for peer in range(1, peers):
                update = update + received[(peer * CORES + c) * slots + s]
            pieces.append(update)
        update = jnp.concatenate(pieces, axis=0)
        value = dot(right[level, 0, s] - update, inverse[level, 0, s])
        live = s < info[3 * level, 0]
        out[level, 0, s] = jnp.where(live, value, jnp.zeros_like(value))


def last_solve(received, column, info, right, inverse, first, mine, theirs):
    return pl.pallas_call(
        functools.partial(last_kernel, right.shape[0] - 1),
        out_shape=jax.ShapeDtypeStruct(right.shape, jnp.float32),
        in_specs=[VMEM, SMEM, SMEM] + [VMEM] * (4 + len(mine)),
        out_specs=VMEM,
        compiler_params=PARAMS,
    )(received, column, info, right, inverse, first, *mine, theirs)


def edge_kernel(level, last, edges, cols, slots, column, *refs):
    infos, couplings, history = refs[:2], refs[2:4], refs[4 : 4 + level]
    out, products = refs[4 + level :]
    core, chip = column[0] % CORES, column[0] // CORES
    chips = cols // CORES
    target_row = (infos[0].shape[0] - 1) // 3
    for c in range(CORES):
        for e in range(edges):
            p = jnp.maximum(infos[c][level - 1, e], 0)
            where = (p // slots) % cols
            there = where // CORES
            other = ((where % CORES) != core).astype(jnp.int32)
            group = (chip + STRIDE - there % STRIDE) % STRIDE
            place = ((group * (chips // STRIDE) + there // STRIDE) * CORES + other) * slots
            place = place + p % slots
            source_level = p // (slots * cols)
            block = history[0][place]
            for index in range(1, level):
                block = jnp.where(source_level == index, history[index][place], block)
            products[c, e] = dot(block, couplings[c][level - 1, 0, e])
    out[...] = jnp.zeros_like(out)
    for c in range(CORES):
        owner = jnp.where(core == c, 0, 1) if last else c
        for e in range(edges):
            goal = infos[c][target_row + level - 1, e]
            live = (goal >= 0).astype(jnp.float32)
            goal = jnp.maximum(goal, 0)
            goal = ((goal // slots) * CORES + owner) * slots + goal % slots
            out[goal] = out[goal] + products[c, e] * live


def edge_terms(level, last, column, infos, couplings, history, row_total, cols, slots):
    edges = couplings[0].shape[2]
    rows, order = history[0].shape[1:]
    return pl.pallas_call(
        functools.partial(edge_kernel, level, last, edges, cols, slots),
        out_shape=jax.ShapeDtypeStruct((row_total * CORES * slots, rows, order), jnp.float32),
        in_specs=[SMEM] * 3 + [VMEM] * (2 + len(history)),
        out_specs=VMEM,
        scratch_shapes=[pltpu.VMEM((CORES, edges, rows, order), jnp.float32)],
        compiler_params=PARAMS,
    )(column, *infos, *couplings, *history)


def swap(x, cols):
    return lax.ppermute(x, "col", [(i, i ^ 1) for i in range(cols)])


def gather_far(solved, cols):
    far = [
        [CORES * (STRIDE * hi + lo) + core for hi in range(cols // CORES // STRIDE)]
        for lo in range(STRIDE)
        for core in range(CORES)
    ]
    return lax.all_gather(solved, "col", axis=0, tiled=False, axis_index_groups=far)


def gather_near(mine, cols):
    def shift(x, k):
        return lax.ppermute(x, "col", [(i, (i + CORES * k) % cols) for i in range(cols)])

    half = mine.shape[0] // 2
    below, above = shift(mine, 1), shift(mine, -1)
    low, high = shift(mine[:half], 2), shift(mine[half:], -2)
    same = jnp.concatenate([mine, below, low, high, above])
    return same.reshape((-1,) + same.shape[2:])


def split_rows(solved, core, cols):
    pairs = [[CORES * chip + core for core in range(CORES)] for chip in range(cols // CORES)]
    both = lax.all_gather(solved, "col", axis=0, tiled=False, axis_index_groups=pairs)
    half = both.shape[2] // CORES
    both = lax.dynamic_slice_in_dim(both, core * half, half, axis=2)
    both = jnp.where(core == 0, both, jnp.flip(both, axis=0))
    return both.reshape((-1,) + both.shape[2:])


def on_device(
    right_sides, inverse_blocks, coupling_blocks, slot_counts, edge_sources, edge_targets
):
    level_total, _, slots = right_sides.shape[:3]
    rows, cols = lax.axis_size("row"), lax.axis_size("col")
    column = lax.axis_index("col").astype(jnp.int32)
    counts = jnp.transpose(slot_counts, (1, 2, 0))
    chip_groups = [
        [row * cols + CORES * chip + core for row in range(rows) for core in range(CORES)]
        for chip in range(cols // CORES)
    ]
    edges = edge_sources.shape[2]
    first = first_solve(counts, right_sides, inverse_blocks)
    solved = split_rows(first, column % CORES, cols)
    column = column.reshape(1)
    history, halves = [], []
    for level in range(1, level_total):
        last = level + 1 == level_total
        mine = gather_far(solved, cols)
        if level == 1:
            coupling, right, inverse, sources, targets, live, mine = lax.optimization_barrier((
                coupling_blocks, right_sides, inverse_blocks, edge_sources, edge_targets,
                slot_counts, mine,
            ))
            couplings = (coupling_blocks, swap(coupling, cols))
            info = jnp.concatenate([
                sources[:, 0], targets[:, 0],
                jnp.broadcast_to(live[:, 0], (level_total, edges)),
            ])
            order = right.shape[-1]
            note = jnp.pad(
                info.astype(jnp.float32), ((0, -info.shape[0] % 8), (0, order - edges))
            )
            packed = swap(jnp.concatenate([
                right[1:-1].reshape(-1, order), inverse[1:-1].reshape(-1, order), note,
            ]), cols)
            other = packed[packed.shape[0] - note.shape[0] :].astype(jnp.int32)
            infos = (info, other[: info.shape[0], :edges])
        if last:
            *blocks, mine = lax.optimization_barrier((*[h[slots:] for h in halves], mine))
            theirs = swap(jnp.stack(blocks), cols)
        history.append(gather_near(mine, cols))
        terms = edge_terms(
            level, last, column, infos, couplings, history, rows, cols, slots
        )
        if last:
            terms, theirs = lax.optimization_barrier((terms, theirs))
            received = lax.all_to_all(
                terms, ("row", "col"), 0, 0, tiled=True, axis_index_groups=chip_groups
            )
            return last_solve(
                received, column, info, right_sides, inverse_blocks, first, halves, theirs
            )
        received = lax.all_to_all(terms, "row", 0, 0, tiled=True)
        solved = half_solve(
            level, received, column, infos, right_sides, inverse_blocks, packed
        )
        halves.append(solved)


def solution(mesh):
    return jax.shard_map(
        on_device,
        mesh=mesh,
        in_specs=(
            P(None, "row", "col", None, None),
            P(None, "row", "col", None, None),
            P(None, "row", "col", None, None),
            P(None, "row", "col"),
            P(None, "row", "col"),
            P(None, "row", "col"),
        ),
        out_specs=P(None, "row", "col", None, None),
        check_vma=False,
    )
```

```python
import functools

import jax
import jax.numpy as jnp
from jax import lax
from jax.experimental import pallas as pl
from jax.experimental.pallas import tpu as pltpu
from jax.sharding import PartitionSpec as P

HIGHEST = lax.Precision.HIGHEST
ANY = pl.BlockSpec(memory_space=pl.ANY)
VMEM = pl.BlockSpec(memory_space=pltpu.VMEM)
SMEM = pl.BlockSpec(memory_space=pltpu.SMEM)
PARAMS = pltpu.CompilerParams(vmem_limit_bytes=16 * 1024 * 1024)
CORES = 2
STRIDE = 4


def dot(a, b):
    return lax.dot_general(
        a, b, (((1,), (0,)), ((), ())), precision=HIGHEST, preferred_element_type=jnp.float32
    )


def first_kernel(counts, right_all, inverse_all, out, right, inverse, sem):
    loads = [
        pltpu.make_async_copy(right_all.at[0, 0], right, sem.at[0]),
        pltpu.make_async_copy(inverse_all.at[0, 0], inverse, sem.at[1]),
    ]
    for load in loads:
        load.start()
    for load in loads:
        load.wait()
    for s in range(right.shape[0]):
        value = dot(right[s], inverse[s])
        out[s] = jnp.where(s < counts[0, 0, 0], value, jnp.zeros_like(value))


def first_solve(counts, right, inverse):
    slots, rows, order = right.shape[2:]
    return pl.pallas_call(
        first_kernel,
        out_shape=jax.ShapeDtypeStruct((slots, rows, order), jnp.float32),
        in_specs=[SMEM, ANY, ANY],
        out_specs=VMEM,
        scratch_shapes=[
            pltpu.VMEM((slots, rows, order), jnp.float32),
            pltpu.VMEM((slots, order, order), jnp.float32),
            pltpu.SemaphoreType.DMA((2,)),
        ],
        compiler_params=pltpu.CompilerParams(vmem_limit_bytes=60 * 1024 * 1024),
    )(counts, right, inverse)


def half_kernel(level, received, column, info, other_info, right, inverse, packed, out):
    levels, _, slots, rows = right.shape[:4]
    half, order = rows // CORES, inverse.shape[3]
    peers = received.shape[0] // (CORES * slots)
    first = pl.multiple_of((column[0] % CORES) * half, half)
    kept = levels - 2
    for c in range(CORES):
        for s in range(slots):
            index = c * slots + s
            update = received[index]
            for peer in range(1, peers):
                update = update + received[peer * CORES * slots + index]
            if c == 0:
                value = right[level, 0, s, pl.ds(first, half), :]
                weight = inverse[level, 0, s]
                count = info[2 * (levels - 1) + level, 0]
            else:
                place = (level - 1) * slots + s
                start = pl.multiple_of(place * rows + first, half)
                value = packed[pl.ds(start, half), :]
                weight = packed[pl.ds(kept * slots * rows + place * order, order), :]
                count = other_info[2 * (levels - 1) + level, 0]
            value = dot(value - update, weight)
            out[index] = jnp.where(s < count, value, jnp.zeros_like(value))


def half_solve(level, received, column, infos, right, inverse, packed):
    slots, rows, order = right.shape[2:]
    return pl.pallas_call(
        functools.partial(half_kernel, level),
        out_shape=jax.ShapeDtypeStruct((CORES * slots, rows // CORES, order), jnp.float32),
        in_specs=[VMEM, SMEM, SMEM, SMEM, VMEM, VMEM, VMEM],
        out_specs=VMEM,
        compiler_params=PARAMS,
    )(received, column, *infos, right, inverse, packed)


def last_kernel(level, received, column, info, right, inverse, first, *refs):
    mine, theirs, out = refs[: level - 1], refs[level - 1], refs[level]
    slots, rows = right.shape[2:4]
    half = rows // CORES
    peers = received.shape[0] // (CORES * slots)
    core = column[0] % CORES
    near = pl.multiple_of(core * half, half)
    away = pl.multiple_of((1 - core) * half, half)
    out[0, 0] = first[...]
    for index in range(1, level):
        for s in range(slots):
            out[index, 0, s, pl.ds(near, half), :] = mine[index - 1][s]
            out[index, 0, s, pl.ds(away, half), :] = theirs[index - 1, s]
    for s in range(slots):
        pieces = []
        for c in range(CORES):
            update = received[c * slots + s]
            for peer in range(1, peers):
                update = update + received[(peer * CORES + c) * slots + s]
            pieces.append(update)
        update = jnp.concatenate(pieces, axis=0)
        value = dot(right[level, 0, s] - update, inverse[level, 0, s])
        live = s < info[3 * level, 0]
        out[level, 0, s] = jnp.where(live, value, jnp.zeros_like(value))


def last_solve(received, column, info, right, inverse, first, mine, theirs):
    return pl.pallas_call(
        functools.partial(last_kernel, right.shape[0] - 1),
        out_shape=jax.ShapeDtypeStruct(right.shape, jnp.float32),
        in_specs=[VMEM, SMEM, SMEM] + [VMEM] * (4 + len(mine)),
        out_specs=VMEM,
        compiler_params=PARAMS,
    )(received, column, info, right, inverse, first, *mine, theirs)


def edge_kernel(level, last, edges, cols, slots, column, *refs):
    infos, couplings, history = refs[:2], refs[2:4], refs[4 : 4 + level]
    out, products = refs[4 + level :]
    core, chip = column[0] % CORES, column[0] // CORES
    chips = cols // CORES
    target_row = (infos[0].shape[0] - 1) // 3
    for c in range(CORES):
        for e in range(edges):
            p = jnp.maximum(infos[c][level - 1, e], 0)
            where = (p // slots) % cols
            there = where // CORES
            other = ((where % CORES) != core).astype(jnp.int32)
            group = (chip + STRIDE - there % STRIDE) % STRIDE
            place = ((group * (chips // STRIDE) + there // STRIDE) * CORES + other) * slots
            place = place + p % slots
            source_level = p // (slots * cols)
            block = history[0][place]
            for index in range(1, level):
                block = jnp.where(source_level == index, history[index][place], block)
            products[c, e] = dot(block, couplings[c][level - 1, 0, e])
    out[...] = jnp.zeros_like(out)
    for c in range(CORES):
        owner = jnp.where(core == c, 0, 1) if last else c
        for e in range(edges):
            goal = infos[c][target_row + level - 1, e]
            live = (goal >= 0).astype(jnp.float32)
            goal = jnp.maximum(goal, 0)
            goal = ((goal // slots) * CORES + owner) * slots + goal % slots
            out[goal] = out[goal] + products[c, e] * live


def edge_terms(level, last, column, infos, couplings, history, row_total, cols, slots):
    edges = couplings[0].shape[2]
    rows, order = history[0].shape[1:]
    return pl.pallas_call(
        functools.partial(edge_kernel, level, last, edges, cols, slots),
        out_shape=jax.ShapeDtypeStruct((row_total * CORES * slots, rows, order), jnp.float32),
        in_specs=[SMEM] * 3 + [VMEM] * (2 + len(history)),
        out_specs=VMEM,
        scratch_shapes=[pltpu.VMEM((CORES, edges, rows, order), jnp.float32)],
        compiler_params=PARAMS,
    )(column, *infos, *couplings, *history)


def swap(x, cols):
    return lax.ppermute(x, "col", [(i, i ^ 1) for i in range(cols)])


def gather_far(solved, cols):
    far = [
        [CORES * (STRIDE * hi + lo) + core for hi in range(cols // CORES // STRIDE)]
        for lo in range(STRIDE)
        for core in range(CORES)
    ]
    return lax.all_gather(solved, "col", axis=0, tiled=False, axis_index_groups=far)


def gather_near(mine, cols):
    def shift(x, even, odd):
        step = (CORES * even, CORES * odd)
        return lax.ppermute(x, "col", [(i, (i + step[i % CORES]) % cols) for i in range(cols)])

    two = shift(mine, 2, -2)
    below, above = shift(mine, 1, 1), shift(mine, -1, -1)
    same = jnp.concatenate([mine, below, two, above])
    return same.reshape((-1,) + same.shape[2:])


def split_rows(solved, core, cols):
    pairs = [[CORES * chip + core for core in range(CORES)] for chip in range(cols // CORES)]
    both = lax.all_gather(solved, "col", axis=0, tiled=False, axis_index_groups=pairs)
    half = both.shape[2] // CORES
    both = lax.dynamic_slice_in_dim(both, core * half, half, axis=2)
    both = jnp.where(core == 0, both, jnp.flip(both, axis=0))
    return both.reshape((-1,) + both.shape[2:])


def on_device(
    right_sides, inverse_blocks, coupling_blocks, slot_counts, edge_sources, edge_targets
):
    level_total, _, slots = right_sides.shape[:3]
    rows, cols = lax.axis_size("row"), lax.axis_size("col")
    column = lax.axis_index("col").astype(jnp.int32)
    counts = jnp.transpose(slot_counts, (1, 2, 0))
    chip_groups = [
        [row * cols + CORES * chip + core for row in range(rows) for core in range(CORES)]
        for chip in range(cols // CORES)
    ]
    edges = edge_sources.shape[2]
    first = first_solve(counts, right_sides, inverse_blocks)
    solved = split_rows(first, column % CORES, cols)
    column = column.reshape(1)
    history, halves = [], []
    for level in range(1, level_total):
        last = level + 1 == level_total
        mine = gather_far(solved, cols)
        if level == 1:
            coupling, right, inverse, sources, targets, live, mine = lax.optimization_barrier((
                coupling_blocks, right_sides, inverse_blocks, edge_sources, edge_targets,
                slot_counts, mine,
            ))
            couplings = (coupling_blocks, swap(coupling, cols))
            info = jnp.concatenate([
                sources[:, 0], targets[:, 0],
                jnp.broadcast_to(live[:, 0], (level_total, edges)),
            ])
            order = right.shape[-1]
            note = jnp.pad(
                info.astype(jnp.float32), ((0, -info.shape[0] % 8), (0, order - edges))
            )
            packed = swap(jnp.concatenate([
                right[1:-1].reshape(-1, order), inverse[1:-1].reshape(-1, order), note,
            ]), cols)
            other = packed[packed.shape[0] - note.shape[0] :].astype(jnp.int32)
            infos = (info, other[: info.shape[0], :edges])
        history.append(gather_near(mine, cols))
        terms = edge_terms(
            level, last, column, infos, couplings, history, rows, cols, slots
        )
        if last:
            blocks = jnp.stack([h[slots:] for h in halves])
            terms, blocks = lax.optimization_barrier((terms, blocks))
            terms, theirs = lax.optimization_barrier((terms, swap(blocks, cols)))
            received = lax.all_to_all(
                terms, ("row", "col"), 0, 0, tiled=True, axis_index_groups=chip_groups
            )
            return last_solve(
                received, column, info, right_sides, inverse_blocks, first, halves, theirs
            )
        received = lax.all_to_all(terms, "row", 0, 0, tiled=True)
        solved = half_solve(
            level, received, column, infos, right_sides, inverse_blocks, packed
        )
        halves.append(solved)


def solution(mesh):
    return jax.shard_map(
        on_device,
        mesh=mesh,
        in_specs=(
            P(None, "row", "col", None, None),
            P(None, "row", "col", None, None),
            P(None, "row", "col", None, None),
            P(None, "row", "col"),
            P(None, "row", "col"),
            P(None, "row", "col"),
        ),
        out_specs=P(None, "row", "col", None, None),
        check_vma=False,
    )
```

```python
import functools

import jax
import jax.numpy as jnp
from jax import lax
from jax.experimental import pallas as pl
from jax.experimental.pallas import tpu as pltpu
from jax.sharding import PartitionSpec as P

HIGHEST = lax.Precision.HIGHEST
ANY = pl.BlockSpec(memory_space=pl.ANY)
VMEM = pl.BlockSpec(memory_space=pltpu.VMEM)
SMEM = pl.BlockSpec(memory_space=pltpu.SMEM)
PARAMS = pltpu.CompilerParams(vmem_limit_bytes=16 * 1024 * 1024)
CORES = 2
STRIDE = 4


def dot(a, b):
    return lax.dot_general(
        a, b, (((1,), (0,)), ((), ())), precision=HIGHEST, preferred_element_type=jnp.float32
    )


def first_kernel(counts, right_all, inverse_all, sources, targets, out, pack, right, inverse, sem):
    levels = right_all.shape[0]
    slots, rows = right.shape[:2]
    order = inverse.shape[1]
    loads = [
        pltpu.make_async_copy(right_all.at[0, 0], right, sem.at[0]),
        pltpu.make_async_copy(inverse_all.at[0, 0], inverse, sem.at[1]),
    ]
    for level in range(1, levels - 1):
        for s in range(slots):
            place = (level - 1) * slots + s
            start = (levels - 2) * slots * rows + place * order
            loads.append(pltpu.make_async_copy(
                right_all.at[level, 0, s], pack.at[pl.ds(place * rows, rows)],
                sem.at[2 * place + 2]))
            loads.append(pltpu.make_async_copy(
                inverse_all.at[level, 0, s], pack.at[pl.ds(start, order)],
                sem.at[2 * place + 3]))
    for load in loads:
        load.start()
    notes = (levels - 2) * slots * (rows + order)
    edges = sources.shape[2]
    pack[notes:, :] = jnp.zeros((pack.shape[0] - notes, order), jnp.float32)
    for level in range(levels - 1):
        pack[pl.ds(notes + level, 1), pl.ds(0, edges)] = sources[level].astype(jnp.float32)
        pack[pl.ds(notes + levels - 1 + level, 1), pl.ds(0, edges)] = (
            targets[level].astype(jnp.float32))
    for level in range(levels):
        pack[pl.ds(notes + 2 * (levels - 1) + level, 1), :] = jnp.full(
            (1, order), counts[0, 0, level].astype(jnp.float32))
    loads[0].wait()
    loads[1].wait()
    for s in range(slots):
        value = dot(right[s], inverse[s])
        out[s] = jnp.where(s < counts[0, 0, 0], value, jnp.zeros_like(value))
    for load in loads[2:]:
        load.wait()


def first_solve(counts, right, inverse, sources, targets):
    levels, _, slots, rows, order = right.shape
    notes = 3 * levels - 2
    packed_rows = (levels - 2) * slots * (rows + order) + notes + -notes % 8
    return pl.pallas_call(
        first_kernel,
        out_shape=(
            jax.ShapeDtypeStruct((slots, rows, order), jnp.float32),
            jax.ShapeDtypeStruct((packed_rows, order), jnp.float32),
        ),
        in_specs=[SMEM, ANY, ANY, VMEM, VMEM],
        out_specs=(VMEM, VMEM),
        scratch_shapes=[
            pltpu.VMEM((slots, rows, order), jnp.float32),
            pltpu.VMEM((slots, order, order), jnp.float32),
            pltpu.SemaphoreType.DMA((2 + 2 * (levels - 2) * slots,)),
        ],
        compiler_params=pltpu.CompilerParams(vmem_limit_bytes=60 * 1024 * 1024),
    )(counts, right, inverse, sources, targets)


def half_kernel(level, levels, slots, received, column, info, other_info, packed, other_packed, out):
    half, order = received.shape[1:]
    rows = half * CORES
    peers = received.shape[0] // (CORES * slots)
    first = pl.multiple_of((column[0] % CORES) * half, half)
    kept = levels - 2
    for c, (notes, data) in enumerate(((info, packed), (other_info, other_packed))):
        for s in range(slots):
            index = c * slots + s
            update = received[index]
            for peer in range(1, peers):
                update = update + received[peer * CORES * slots + index]
            place = (level - 1) * slots + s
            start = pl.multiple_of(place * rows + first, half)
            value = data[pl.ds(start, half), :]
            weight = data[pl.ds(kept * slots * rows + place * order, order), :]
            value = dot(value - update, weight)
            live = s < notes[2 * (levels - 1) + level, 0]
            out[index] = jnp.where(live, value, jnp.zeros_like(value))


def half_solve(level, levels, slots, received, column, infos, packs):
    half, order = received.shape[1:]
    return pl.pallas_call(
        functools.partial(half_kernel, level, levels, slots),
        out_shape=jax.ShapeDtypeStruct((CORES * slots, half, order), jnp.float32),
        in_specs=[VMEM, SMEM, SMEM, SMEM, VMEM, VMEM],
        out_specs=VMEM,
        compiler_params=PARAMS,
    )(received, column, *infos, *packs)


def last_kernel(level, received, column, info, right, inverse, first, *refs):
    mine, theirs, out = refs[: level - 1], refs[level - 1], refs[level]
    slots, rows = right.shape[2:4]
    half = rows // CORES
    peers = received.shape[0] // (CORES * slots)
    core = column[0] % CORES
    near = pl.multiple_of(core * half, half)
    away = pl.multiple_of((1 - core) * half, half)
    out[0, 0] = first[...]
    for index in range(1, level):
        for s in range(slots):
            out[index, 0, s, pl.ds(near, half), :] = mine[index - 1][s]
            out[index, 0, s, pl.ds(away, half), :] = theirs[index - 1, s]
    for s in range(slots):
        pieces = []
        for c in range(CORES):
            update = received[c * slots + s]
            for peer in range(1, peers):
                update = update + received[(peer * CORES + c) * slots + s]
            pieces.append(update)
        update = jnp.concatenate(pieces, axis=0)
        value = dot(right[level, 0, s] - update, inverse[level, 0, s])
        live = s < info[3 * level, 0]
        out[level, 0, s] = jnp.where(live, value, jnp.zeros_like(value))


def last_solve(received, column, info, right, inverse, first, mine, theirs):
    return pl.pallas_call(
        functools.partial(last_kernel, right.shape[0] - 1),
        out_shape=jax.ShapeDtypeStruct(right.shape, jnp.float32),
        in_specs=[VMEM, SMEM, SMEM] + [VMEM] * (4 + len(mine)),
        out_specs=VMEM,
        compiler_params=PARAMS,
    )(received, column, info, right, inverse, first, *mine, theirs)


def edge_kernel(level, last, edges, cols, slots, column, *refs):
    infos, couplings, history = refs[:2], refs[2:4], refs[4 : 4 + level]
    out, products = refs[4 + level :]
    core, chip = column[0] % CORES, column[0] // CORES
    chips = cols // CORES
    target_row = (infos[0].shape[0] - 1) // 3
    for c in range(CORES):
        for e in range(edges):
            p = jnp.maximum(infos[c][level - 1, e], 0)
            where = (p // slots) % cols
            there = where // CORES
            other = ((where % CORES) != core).astype(jnp.int32)
            group = (chip + STRIDE - there % STRIDE) % STRIDE
            place = ((group * (chips // STRIDE) + there // STRIDE) * CORES + other) * slots
            place = place + p % slots
            source_level = p // (slots * cols)
            block = history[0][place]
            for index in range(1, level):
                block = jnp.where(source_level == index, history[index][place], block)
            products[c, e] = dot(block, couplings[c][level - 1, 0, e])
    out[...] = jnp.zeros_like(out)
    for c in range(CORES):
        owner = jnp.where(core == c, 0, 1) if last else c
        for e in range(edges):
            goal = infos[c][target_row + level - 1, e]
            live = (goal >= 0).astype(jnp.float32)
            goal = jnp.maximum(goal, 0)
            goal = ((goal // slots) * CORES + owner) * slots + goal % slots
            out[goal] = out[goal] + products[c, e] * live


def edge_terms(level, last, column, infos, couplings, history, row_total, cols, slots):
    edges = couplings[0].shape[2]
    rows, order = history[0].shape[1:]
    return pl.pallas_call(
        functools.partial(edge_kernel, level, last, edges, cols, slots),
        out_shape=jax.ShapeDtypeStruct((row_total * CORES * slots, rows, order), jnp.float32),
        in_specs=[SMEM] * 3 + [VMEM] * (2 + len(history)),
        out_specs=VMEM,
        scratch_shapes=[pltpu.VMEM((CORES, edges, rows, order), jnp.float32)],
        compiler_params=PARAMS,
    )(column, *infos, *couplings, *history)


def swap(x, cols):
    return lax.ppermute(x, "col", [(i, i ^ 1) for i in range(cols)])


def gather_far(solved, cols):
    far = [
        [CORES * (STRIDE * hi + lo) + core for hi in range(cols // CORES // STRIDE)]
        for lo in range(STRIDE)
        for core in range(CORES)
    ]
    return lax.all_gather(solved, "col", axis=0, tiled=False, axis_index_groups=far)


def gather_near(mine, cols):
    def shift(x, even, odd):
        step = (CORES * even, CORES * odd)
        return lax.ppermute(x, "col", [(i, (i + step[i % CORES]) % cols) for i in range(cols)])

    two = shift(mine, 2, -2)
    below, above = shift(mine, 1, 1), shift(mine, -1, -1)
    same = jnp.concatenate([mine, below, two, above])
    return same.reshape((-1,) + same.shape[2:])


def split_rows(solved, core, cols):
    pairs = [[CORES * chip + core for core in range(CORES)] for chip in range(cols // CORES)]
    both = lax.all_gather(solved, "col", axis=0, tiled=False, axis_index_groups=pairs)
    half = both.shape[2] // CORES
    both = lax.dynamic_slice_in_dim(both, core * half, half, axis=2)
    both = jnp.where(core == 0, both, jnp.flip(both, axis=0))
    return both.reshape((-1,) + both.shape[2:])


def on_device(
    right_sides, inverse_blocks, coupling_blocks, slot_counts, edge_sources, edge_targets
):
    level_total, _, slots = right_sides.shape[:3]
    rows, cols = lax.axis_size("row"), lax.axis_size("col")
    column = lax.axis_index("col").astype(jnp.int32)
    counts = jnp.transpose(slot_counts, (1, 2, 0))
    chip_groups = [
        [row * cols + CORES * chip + core for row in range(rows) for core in range(CORES)]
        for chip in range(cols // CORES)
    ]
    edges = edge_sources.shape[2]
    first, pack = first_solve(
        counts, right_sides, inverse_blocks, edge_sources, edge_targets
    )
    solved = split_rows(first, column % CORES, cols)
    column = column.reshape(1)
    history, halves = [], []
    for level in range(1, level_total):
        last = level + 1 == level_total
        mine = gather_far(solved, cols)
        if level == 1:
            coupling, pack, mine = lax.optimization_barrier((coupling_blocks, pack, mine))
            couplings = (coupling_blocks, swap(coupling, cols))
            packs = (pack, swap(pack, cols))
            notes = 3 * level_total - 2
            start = pack.shape[0] - notes - -notes % 8
            infos = tuple(
                block[start : start + notes, :edges].astype(jnp.int32) for block in packs
            )
        history.append(gather_near(mine, cols))
        terms = edge_terms(
            level, last, column, infos, couplings, history, rows, cols, slots
        )
        if last:
            blocks = jnp.stack([h[slots:] for h in halves])
            terms, blocks = lax.optimization_barrier((terms, blocks))
            terms, theirs = lax.optimization_barrier((terms, swap(blocks, cols)))
            received = lax.all_to_all(
                terms, ("row", "col"), 0, 0, tiled=True, axis_index_groups=chip_groups
            )
            return last_solve(
                received, column, infos[0], right_sides, inverse_blocks, first, halves, theirs
            )
        received = lax.all_to_all(terms, "row", 0, 0, tiled=True)
        solved = half_solve(
            level, level_total, slots, received, column, infos, packs
        )
        halves.append(solved)


def solution(mesh):
    return jax.shard_map(
        on_device,
        mesh=mesh,
        in_specs=(
            P(None, "row", "col", None, None),
            P(None, "row", "col", None, None),
            P(None, "row", "col", None, None),
            P(None, "row", "col"),
            P(None, "row", "col"),
            P(None, "row", "col"),
        ),
        out_specs=P(None, "row", "col", None, None),
        check_vma=False,
    )
```

```python
import functools

import jax
import jax.numpy as jnp
from jax import lax
from jax.experimental import pallas as pl
from jax.experimental.pallas import tpu as pltpu
from jax.sharding import PartitionSpec as P

HIGHEST = lax.Precision.HIGHEST
ANY = pl.BlockSpec(memory_space=pl.ANY)
VMEM = pl.BlockSpec(memory_space=pltpu.VMEM)
SMEM = pl.BlockSpec(memory_space=pltpu.SMEM)
PARAMS = pltpu.CompilerParams(vmem_limit_bytes=16 * 1024 * 1024)
CORES = 2
STRIDE = 4


def dot(a, b):
    return lax.dot_general(
        a, b, (((1,), (0,)), ((), ())), precision=HIGHEST, preferred_element_type=jnp.float32
    )


def first_kernel(counts, right_all, inverse_all, sources, targets, out, pack, right, inverse, sem):
    levels = right_all.shape[0]
    slots, rows = right.shape[:2]
    order = inverse.shape[1]
    loads = [
        pltpu.make_async_copy(right_all.at[0, 0], right, sem.at[0]),
        pltpu.make_async_copy(inverse_all.at[0, 0], inverse, sem.at[1]),
    ]
    for level in range(1, levels - 1):
        for s in range(slots):
            place = (level - 1) * slots + s
            start = (levels - 2) * slots * rows + place * order
            loads.append(pltpu.make_async_copy(
                right_all.at[level, 0, s], pack.at[pl.ds(place * rows, rows)],
                sem.at[2 * place + 2]))
            loads.append(pltpu.make_async_copy(
                inverse_all.at[level, 0, s], pack.at[pl.ds(start, order)],
                sem.at[2 * place + 3]))
    for load in loads:
        load.start()
    notes = (levels - 2) * slots * (rows + order)
    edges = sources.shape[2]
    pack[notes:, :] = jnp.zeros((pack.shape[0] - notes, order), jnp.float32)
    for level in range(levels - 1):
        pack[pl.ds(notes + level, 1), pl.ds(0, edges)] = sources[level].astype(jnp.float32)
        pack[pl.ds(notes + levels - 1 + level, 1), pl.ds(0, edges)] = (
            targets[level].astype(jnp.float32))
    for level in range(levels):
        pack[pl.ds(notes + 2 * (levels - 1) + level, 1), :] = jnp.full(
            (1, order), counts[0, 0, level].astype(jnp.float32))
    loads[0].wait()
    loads[1].wait()
    for s in range(slots):
        value = dot(right[s], inverse[s])
        out[s] = jnp.where(s < counts[0, 0, 0], value, jnp.zeros_like(value))
    for load in loads[2:]:
        load.wait()


def first_solve(counts, right, inverse, sources, targets):
    levels, _, slots, rows, order = right.shape
    notes = 3 * levels - 2
    packed_rows = (levels - 2) * slots * (rows + order) + notes + -notes % 8
    return pl.pallas_call(
        first_kernel,
        out_shape=(
            jax.ShapeDtypeStruct((slots, rows, order), jnp.float32),
            jax.ShapeDtypeStruct((packed_rows, order), jnp.float32),
        ),
        in_specs=[SMEM, ANY, ANY, VMEM, VMEM],
        out_specs=(VMEM, VMEM),
        scratch_shapes=[
            pltpu.VMEM((slots, rows, order), jnp.float32),
            pltpu.VMEM((slots, order, order), jnp.float32),
            pltpu.SemaphoreType.DMA((2 + 2 * (levels - 2) * slots,)),
        ],
        compiler_params=pltpu.CompilerParams(vmem_limit_bytes=60 * 1024 * 1024),
    )(counts, right, inverse, sources, targets)


def half_kernel(level, levels, slots, received, column, info, other_info, packed, other_packed, out):
    half, order = received.shape[1:]
    rows = half * CORES
    peers = received.shape[0] // (CORES * slots)
    first = pl.multiple_of((column[0] % CORES) * half, half)
    kept = levels - 2
    for c, (notes, data) in enumerate(((info, packed), (other_info, other_packed))):
        for s in range(slots):
            index = c * slots + s
            update = received[index]
            for peer in range(1, peers):
                update = update + received[peer * CORES * slots + index]
            place = (level - 1) * slots + s
            start = pl.multiple_of(place * rows + first, half)
            value = data[pl.ds(start, half), :]
            weight = data[pl.ds(kept * slots * rows + place * order, order), :]
            value = dot(value - update, weight)
            live = s < notes[2 * (levels - 1) + level, 0]
            out[index] = jnp.where(live, value, jnp.zeros_like(value))


def half_solve(level, levels, slots, received, column, infos, packs):
    half, order = received.shape[1:]
    return pl.pallas_call(
        functools.partial(half_kernel, level, levels, slots),
        out_shape=jax.ShapeDtypeStruct((CORES * slots, half, order), jnp.float32),
        in_specs=[VMEM, SMEM, SMEM, SMEM, VMEM, VMEM],
        out_specs=VMEM,
        compiler_params=PARAMS,
    )(received, column, *infos, *packs)


def last_kernel(level, received, column, info, right, inverse, first, *refs):
    mine, theirs, out = refs[: level - 1], refs[level - 1], refs[level]
    slots, rows = right.shape[2:4]
    half = rows // CORES
    peers = received.shape[0] // (CORES * slots)
    core = column[0] % CORES
    near = pl.multiple_of(core * half, half)
    away = pl.multiple_of((1 - core) * half, half)
    out[0, 0] = first[...]
    for index in range(1, level):
        for s in range(slots):
            out[index, 0, s, pl.ds(near, half), :] = mine[index - 1][s]
            out[index, 0, s, pl.ds(away, half), :] = theirs[index - 1, s]
    for s in range(slots):
        pieces = []
        for c in range(CORES):
            update = received[c * slots + s]
            for peer in range(1, peers):
                update = update + received[(peer * CORES + c) * slots + s]
            pieces.append(update)
        update = jnp.concatenate(pieces, axis=0)
        value = dot(right[level, 0, s] - update, inverse[level, 0, s])
        live = s < info[3 * level, 0]
        out[level, 0, s] = jnp.where(live, value, jnp.zeros_like(value))


def last_solve(received, column, info, right, inverse, first, mine, theirs):
    return pl.pallas_call(
        functools.partial(last_kernel, right.shape[0] - 1),
        out_shape=jax.ShapeDtypeStruct(right.shape, jnp.float32),
        in_specs=[VMEM, SMEM, SMEM] + [VMEM] * (4 + len(mine)),
        out_specs=VMEM,
        compiler_params=PARAMS,
    )(received, column, info, right, inverse, first, *mine, theirs)


def edge_kernel(level, last, edges, cols, slots, column, *refs):
    infos, couplings, history = refs[:2], refs[2:4], refs[4 : 4 + level]
    out, products = refs[4 + level :]
    core, chip = column[0] % CORES, column[0] // CORES
    chips = cols // CORES
    target_row = (infos[0].shape[0] - 1) // 3
    for c in range(CORES):
        for e in range(edges):
            p = jnp.maximum(infos[c][level - 1, e], 0)
            where = (p // slots) % cols
            there = where // CORES
            other = ((where % CORES) != core).astype(jnp.int32)
            group = (chip + STRIDE - there % STRIDE) % STRIDE
            place = ((group * (chips // STRIDE) + there // STRIDE) * CORES + other) * slots
            place = place + p % slots
            source_level = p // (slots * cols)
            block = history[0][place]
            for index in range(1, level):
                block = jnp.where(source_level == index, history[index][place], block)
            products[c, e] = dot(block, couplings[c][level - 1, 0, e])
    out[...] = jnp.zeros_like(out)
    for c in range(CORES):
        owner = jnp.where(core == c, 0, 1) if last else c
        for e in range(edges):
            goal = infos[c][target_row + level - 1, e]
            live = (goal >= 0).astype(jnp.float32)
            goal = jnp.maximum(goal, 0)
            goal = ((goal // slots) * CORES + owner) * slots + goal % slots
            out[goal] = out[goal] + products[c, e] * live


def edge_terms(level, last, column, infos, couplings, history, row_total, cols, slots):
    edges = couplings[0].shape[2]
    rows, order = history[0].shape[1:]
    return pl.pallas_call(
        functools.partial(edge_kernel, level, last, edges, cols, slots),
        out_shape=jax.ShapeDtypeStruct((row_total * CORES * slots, rows, order), jnp.float32),
        in_specs=[SMEM] * 3 + [VMEM] * (2 + len(history)),
        out_specs=VMEM,
        scratch_shapes=[pltpu.VMEM((CORES, edges, rows, order), jnp.float32)],
        compiler_params=PARAMS,
    )(column, *infos, *couplings, *history)


def swap(x, cols):
    return lax.ppermute(x, "col", [(i, i ^ 1) for i in range(cols)])


def gather_far(solved, cols):
    far = [
        [CORES * (STRIDE * hi + lo) + core for hi in range(cols // CORES // STRIDE)]
        for lo in range(STRIDE)
        for core in range(CORES)
    ]
    return lax.all_gather(solved, "col", axis=0, tiled=False, axis_index_groups=far)


def gather_near(mine, cols):
    def shift(x, k):
        return lax.ppermute(x, "col", [(i, (i + CORES * k) % cols) for i in range(cols)])

    half = mine.shape[0] // 2
    below, above = shift(mine, 1), shift(mine, -1)
    low, high = shift(mine[:half], 2), shift(mine[half:], -2)
    same = jnp.concatenate([mine, below, low, high, above])
    return same.reshape((-1,) + same.shape[2:])


def split_rows(solved, core, cols):
    pairs = [[CORES * chip + core for core in range(CORES)] for chip in range(cols // CORES)]
    both = lax.all_gather(solved, "col", axis=0, tiled=False, axis_index_groups=pairs)
    half = both.shape[2] // CORES
    both = lax.dynamic_slice_in_dim(both, core * half, half, axis=2)
    both = jnp.where(core == 0, both, jnp.flip(both, axis=0))
    return both.reshape((-1,) + both.shape[2:])


def on_device(
    right_sides, inverse_blocks, coupling_blocks, slot_counts, edge_sources, edge_targets
):
    level_total, _, slots = right_sides.shape[:3]
    rows, cols = lax.axis_size("row"), lax.axis_size("col")
    column = lax.axis_index("col").astype(jnp.int32)
    counts = jnp.transpose(slot_counts, (1, 2, 0))
    chip_groups = [
        [row * cols + CORES * chip + core for row in range(rows) for core in range(CORES)]
        for chip in range(cols // CORES)
    ]
    edges = edge_sources.shape[2]
    first, pack = first_solve(
        counts, right_sides, inverse_blocks, edge_sources, edge_targets
    )
    solved = split_rows(first, column % CORES, cols)
    column = column.reshape(1)
    history, halves = [], []
    for level in range(1, level_total):
        last = level + 1 == level_total
        mine = gather_far(solved, cols)
        if level == 1:
            coupling, pack, mine = lax.optimization_barrier((coupling_blocks, pack, mine))
            couplings = (coupling_blocks, swap(coupling, cols))
            packs = (pack, swap(pack, cols))
            notes = 3 * level_total - 2
            start = pack.shape[0] - notes - -notes % 8
            infos = tuple(
                block[start : start + notes, :edges].astype(jnp.int32) for block in packs
            )
        history.append(gather_near(mine, cols))
        terms = edge_terms(
            level, last, column, infos, couplings, history, rows, cols, slots
        )
        if last:
            blocks = jnp.stack([h[slots:] for h in halves])
            terms, blocks = lax.optimization_barrier((terms, blocks))
            terms, theirs = lax.optimization_barrier((terms, swap(blocks, cols)))
            received = lax.all_to_all(
                terms, ("row", "col"), 0, 0, tiled=True, axis_index_groups=chip_groups
            )
            return last_solve(
                received, column, infos[0], right_sides, inverse_blocks, first, halves, theirs
            )
        received = lax.all_to_all(terms, "row", 0, 0, tiled=True)
        solved = half_solve(
            level, level_total, slots, received, column, infos, packs
        )
        halves.append(solved)


def solution(mesh):
    return jax.shard_map(
        on_device,
        mesh=mesh,
        in_specs=(
            P(None, "row", "col", None, None),
            P(None, "row", "col", None, None),
            P(None, "row", "col", None, None),
            P(None, "row", "col"),
            P(None, "row", "col"),
            P(None, "row", "col"),
        ),
        out_specs=P(None, "row", "col", None, None),
        check_vma=False,
    )
```

```python
import functools

import jax
import jax.numpy as jnp
from jax import lax
from jax.experimental import pallas as pl
from jax.experimental.pallas import tpu as pltpu
from jax.sharding import PartitionSpec as P

HIGHEST = lax.Precision.HIGHEST
ANY = pl.BlockSpec(memory_space=pl.ANY)
VMEM = pl.BlockSpec(memory_space=pltpu.VMEM)
SMEM = pl.BlockSpec(memory_space=pltpu.SMEM)
PARAMS = pltpu.CompilerParams(vmem_limit_bytes=16 * 1024 * 1024)
CORES = 2
STRIDE = 4


def dot(a, b):
    return lax.dot_general(
        a, b, (((1,), (0,)), ((), ())), precision=HIGHEST, preferred_element_type=jnp.float32
    )


def first_kernel(counts, right_all, inverse_all, sources, targets, out, pack, right, inverse, sem):
    levels = right_all.shape[0]
    slots, rows = right.shape[:2]
    order = inverse.shape[1]
    loads = [
        pltpu.make_async_copy(right_all.at[0, 0], right, sem.at[0]),
        pltpu.make_async_copy(inverse_all.at[0, 0], inverse, sem.at[1]),
    ]
    for level in range(1, levels - 1):
        for s in range(slots):
            place = (level - 1) * slots + s
            start = (levels - 2) * slots * rows + place * order
            loads.append(pltpu.make_async_copy(
                right_all.at[level, 0, s], pack.at[pl.ds(place * rows, rows)],
                sem.at[2 * place + 2]))
            loads.append(pltpu.make_async_copy(
                inverse_all.at[level, 0, s], pack.at[pl.ds(start, order)],
                sem.at[2 * place + 3]))
    for load in loads:
        load.start()
    notes = (levels - 2) * slots * (rows + order)
    edges = sources.shape[2]
    pack[notes:, :] = jnp.zeros((pack.shape[0] - notes, order), jnp.float32)
    for level in range(levels - 1):
        pack[pl.ds(notes + level, 1), pl.ds(0, edges)] = sources[level].astype(jnp.float32)
        pack[pl.ds(notes + levels - 1 + level, 1), pl.ds(0, edges)] = (
            targets[level].astype(jnp.float32))
    for level in range(levels):
        pack[pl.ds(notes + 2 * (levels - 1) + level, 1), :] = jnp.full(
            (1, order), counts[0, 0, level].astype(jnp.float32))
    loads[0].wait()
    loads[1].wait()
    for s in range(slots):
        value = dot(right[s], inverse[s])
        out[s] = jnp.where(s < counts[0, 0, 0], value, jnp.zeros_like(value))
    for load in loads[2:]:
        load.wait()


def first_solve(counts, right, inverse, sources, targets):
    levels, _, slots, rows, order = right.shape
    notes = 3 * levels - 2
    packed_rows = (levels - 2) * slots * (rows + order) + notes + -notes % 8
    return pl.pallas_call(
        first_kernel,
        out_shape=(
            jax.ShapeDtypeStruct((slots, rows, order), jnp.float32),
            jax.ShapeDtypeStruct((packed_rows, order), jnp.float32),
        ),
        in_specs=[SMEM, ANY, ANY, VMEM, VMEM],
        out_specs=(VMEM, VMEM),
        scratch_shapes=[
            pltpu.VMEM((slots, rows, order), jnp.float32),
            pltpu.VMEM((slots, order, order), jnp.float32),
            pltpu.SemaphoreType.DMA((2 + 2 * (levels - 2) * slots,)),
        ],
        compiler_params=pltpu.CompilerParams(vmem_limit_bytes=60 * 1024 * 1024),
    )(counts, right, inverse, sources, targets)


def half_kernel(level, levels, slots, received, column, info, other_info, packed, other_packed, out):
    half, order = received.shape[1:]
    rows = half * CORES
    peers = received.shape[0] // (CORES * slots)
    first = pl.multiple_of((column[0] % CORES) * half, half)
    kept = levels - 2
    for c, (notes, data) in enumerate(((info, packed), (other_info, other_packed))):
        for s in range(slots):
            index = c * slots + s
            update = received[index]
            for peer in range(1, peers):
                update = update + received[peer * CORES * slots + index]
            place = (level - 1) * slots + s
            start = pl.multiple_of(place * rows + first, half)
            value = data[pl.ds(start, half), :]
            weight = data[pl.ds(kept * slots * rows + place * order, order), :]
            value = dot(value - update, weight)
            live = s < notes[2 * (levels - 1) + level, 0]
            out[index] = jnp.where(live, value, jnp.zeros_like(value))


def half_solve(level, levels, slots, received, column, infos, packs):
    half, order = received.shape[1:]
    return pl.pallas_call(
        functools.partial(half_kernel, level, levels, slots),
        out_shape=jax.ShapeDtypeStruct((CORES * slots, half, order), jnp.float32),
        in_specs=[VMEM, SMEM, SMEM, SMEM, VMEM, VMEM],
        out_specs=VMEM,
        compiler_params=PARAMS,
    )(received, column, *infos, *packs)


def last_kernel(level, received, column, info, right, inverse, first, *refs):
    mine, theirs, out = refs[: level - 1], refs[level - 1], refs[level]
    slots, rows = right.shape[2:4]
    half = rows // CORES
    peers = received.shape[0] // (CORES * slots)
    core = column[0] % CORES
    near = pl.multiple_of(core * half, half)
    away = pl.multiple_of((1 - core) * half, half)
    out[0, 0] = first[...]
    for index in range(1, level):
        for s in range(slots):
            out[index, 0, s, pl.ds(near, half), :] = mine[index - 1][s]
            out[index, 0, s, pl.ds(away, half), :] = theirs[index - 1, s]
    for s in range(slots):
        pieces = []
        for c in range(CORES):
            update = received[c * slots + s]
            for peer in range(1, peers):
                update = update + received[(peer * CORES + c) * slots + s]
            pieces.append(update)
        update = jnp.concatenate(pieces, axis=0)
        value = dot(right[level, 0, s] - update, inverse[level, 0, s])
        live = s < info[3 * level, 0]
        out[level, 0, s] = jnp.where(live, value, jnp.zeros_like(value))


def last_solve(received, column, info, right, inverse, first, mine, theirs):
    return pl.pallas_call(
        functools.partial(last_kernel, right.shape[0] - 1),
        out_shape=jax.ShapeDtypeStruct(right.shape, jnp.float32),
        in_specs=[VMEM, SMEM, SMEM] + [VMEM] * (4 + len(mine)),
        out_specs=VMEM,
        compiler_params=PARAMS,
    )(received, column, info, right, inverse, first, *mine, theirs)


def edge_kernel(level, last, edges, cols, slots, column, *refs):
    infos, couplings, history = refs[:2], refs[2:4], refs[4 : 4 + level]
    out, products = refs[4 + level :]
    core, chip = column[0] % CORES, column[0] // CORES
    chips = cols // CORES
    target_row = (infos[0].shape[0] - 1) // 3
    for c in range(CORES):
        for e in range(edges):
            p = jnp.maximum(infos[c][level - 1, e], 0)
            where = (p // slots) % cols
            there = where // CORES
            other = ((where % CORES) != core).astype(jnp.int32)
            group = (chip + STRIDE - there % STRIDE) % STRIDE
            place = ((group * (chips // STRIDE) + there // STRIDE) * CORES + other) * slots
            place = place + p % slots
            source_level = p // (slots * cols)
            block = history[0][place]
            for index in range(1, level):
                block = jnp.where(source_level == index, history[index][place], block)
            products[c, e] = dot(block, couplings[c][level - 1, 0, e])
    out[...] = jnp.zeros_like(out)
    for c in range(CORES):
        owner = jnp.where(core == c, 0, 1) if last else c
        for e in range(edges):
            goal = infos[c][target_row + level - 1, e]
            live = (goal >= 0).astype(jnp.float32)
            goal = jnp.maximum(goal, 0)
            goal = ((goal // slots) * CORES + owner) * slots + goal % slots
            out[goal] = out[goal] + products[c, e] * live


def edge_terms(level, last, column, infos, couplings, history, row_total, cols, slots):
    edges = couplings[0].shape[2]
    rows, order = history[0].shape[1:]
    return pl.pallas_call(
        functools.partial(edge_kernel, level, last, edges, cols, slots),
        out_shape=jax.ShapeDtypeStruct((row_total * CORES * slots, rows, order), jnp.float32),
        in_specs=[SMEM] * 3 + [VMEM] * (2 + len(history)),
        out_specs=VMEM,
        scratch_shapes=[pltpu.VMEM((CORES, edges, rows, order), jnp.float32)],
        compiler_params=PARAMS,
    )(column, *infos, *couplings, *history)


def swap(x, cols):
    return lax.ppermute(x, "col", [(i, i ^ 1) for i in range(cols)])


def gather_far(solved, cols):
    far = [
        [CORES * (STRIDE * hi + lo) + core for hi in range(cols // CORES // STRIDE)]
        for lo in range(STRIDE)
        for core in range(CORES)
    ]
    return lax.all_gather(solved, "col", axis=0, tiled=False, axis_index_groups=far)


def gather_near(mine, cols):
    def shift(x, k):
        return lax.ppermute(x, "col", [(i, (i + CORES * k) % cols) for i in range(cols)])

    half = mine.shape[0] // 2
    below, above = shift(mine, 1), shift(mine, -1)
    low, high = shift(mine[:half], 2), shift(mine[half:], -2)
    same = jnp.concatenate([mine, below, low, high, above])
    return same.reshape((-1,) + same.shape[2:])


def split_rows(solved, core, cols):
    pairs = [[CORES * chip + core for core in range(CORES)] for chip in range(cols // CORES)]
    both = lax.all_gather(solved, "col", axis=0, tiled=False, axis_index_groups=pairs)
    half = both.shape[2] // CORES
    both = lax.dynamic_slice_in_dim(both, core * half, half, axis=2)
    both = jnp.where(core == 0, both, jnp.flip(both, axis=0))
    return both.reshape((-1,) + both.shape[2:])


def on_device(
    right_sides, inverse_blocks, coupling_blocks, slot_counts, edge_sources, edge_targets
):
    level_total, _, slots = right_sides.shape[:3]
    rows, cols = lax.axis_size("row"), lax.axis_size("col")
    column = lax.axis_index("col").astype(jnp.int32)
    counts = jnp.transpose(slot_counts, (1, 2, 0))
    chip_groups = [
        [row * cols + CORES * chip + core for row in range(rows) for core in range(CORES)]
        for chip in range(cols // CORES)
    ]
    edges = edge_sources.shape[2]
    first, pack = first_solve(
        counts, right_sides, inverse_blocks, edge_sources, edge_targets
    )
    solved = split_rows(first, column % CORES, cols)
    column = column.reshape(1)
    history, halves = [], []
    for level in range(1, level_total):
        last = level + 1 == level_total
        if level == 1:
            coupling, pack, solved = lax.optimization_barrier((coupling_blocks, pack, solved))
            couplings = (coupling_blocks, swap(coupling, cols))
            packs = (pack, swap(pack, cols))
            notes = 3 * level_total - 2
            start = pack.shape[0] - notes - -notes % 8
            infos = tuple(
                block[start : start + notes, :edges].astype(jnp.int32) for block in packs
            )
        mine = gather_far(solved, cols)
        history.append(gather_near(mine, cols))
        terms = edge_terms(
            level, last, column, infos, couplings, history, rows, cols, slots
        )
        if last:
            blocks = jnp.stack([h[slots:] for h in halves])
            terms, blocks = lax.optimization_barrier((terms, blocks))
            terms, theirs = lax.optimization_barrier((terms, swap(blocks, cols)))
            received = lax.all_to_all(
                terms, ("row", "col"), 0, 0, tiled=True, axis_index_groups=chip_groups
            )
            return last_solve(
                received, column, infos[0], right_sides, inverse_blocks, first, halves, theirs
            )
        received = lax.all_to_all(terms, "row", 0, 0, tiled=True)
        solved = half_solve(
            level, level_total, slots, received, column, infos, packs
        )
        halves.append(solved)


def solution(mesh):
    return jax.shard_map(
        on_device,
        mesh=mesh,
        in_specs=(
            P(None, "row", "col", None, None),
            P(None, "row", "col", None, None),
            P(None, "row", "col", None, None),
            P(None, "row", "col"),
            P(None, "row", "col"),
            P(None, "row", "col"),
        ),
        out_specs=P(None, "row", "col", None, None),
        check_vma=False,
    )
```

```python
import functools

import jax
import jax.numpy as jnp
from jax import lax
from jax.experimental import pallas as pl
from jax.experimental.pallas import tpu as pltpu
from jax.sharding import PartitionSpec as P

HIGHEST = lax.Precision.HIGHEST
ANY = pl.BlockSpec(memory_space=pl.ANY)
VMEM = pl.BlockSpec(memory_space=pltpu.VMEM)
SMEM = pl.BlockSpec(memory_space=pltpu.SMEM)
PARAMS = pltpu.CompilerParams(vmem_limit_bytes=32 * 1024 * 1024)
CORES = 2
STRIDE = 4


def dot(a, b):
    return lax.dot_general(
        a, b, (((1,), (0,)), ((), ())), precision=HIGHEST, preferred_element_type=jnp.float32
    )


def first_kernel(counts, right_all, inverse_all, out, right, inverse, sem):
    loads = [
        pltpu.make_async_copy(right_all.at[0, 0], right, sem.at[0]),
        pltpu.make_async_copy(inverse_all.at[0, 0], inverse, sem.at[1]),
    ]
    for load in loads:
        load.start()
    for load in loads:
        load.wait()
    for s in range(right.shape[0]):
        value = dot(right[s], inverse[s])
        out[s] = jnp.where(s < counts[0, 0, 0], value, jnp.zeros_like(value))


def first_solve(counts, right, inverse):
    slots, rows, order = right.shape[2:]
    return pl.pallas_call(
        first_kernel,
        out_shape=jax.ShapeDtypeStruct((slots, rows, order), jnp.float32),
        in_specs=[SMEM, ANY, ANY],
        out_specs=VMEM,
        scratch_shapes=[
            pltpu.VMEM((slots, rows, order), jnp.float32),
            pltpu.VMEM((slots, order, order), jnp.float32),
            pltpu.SemaphoreType.DMA((2,)),
        ],
        compiler_params=pltpu.CompilerParams(vmem_limit_bytes=60 * 1024 * 1024),
    )(counts, right, inverse)


def half_kernel(level, received, column, info, other_info, right, inverse, packed, out):
    levels, _, slots, rows = right.shape[:4]
    half, order = rows // CORES, inverse.shape[3]
    peers = received.shape[0] // (CORES * slots)
    first = pl.multiple_of((column[0] % CORES) * half, half)
    kept = levels - 2
    for c in range(CORES):
        for s in range(slots):
            index = c * slots + s
            update = received[index]
            for peer in range(1, peers):
                update = update + received[peer * CORES * slots + index]
            if c == 0:
                value = right[level, 0, s, pl.ds(first, half), :]
                weight = inverse[level, 0, s]
                count = info[2 * (levels - 1) + level, 0]
            else:
                place = (level - 1) * slots + s
                start = pl.multiple_of(place * rows + first, half)
                value = packed[pl.ds(start, half), :]
                weight = packed[pl.ds(kept * slots * rows + place * order, order), :]
                count = other_info[2 * (levels - 1) + level, 0]
            value = dot(value - update, weight)
            out[index] = jnp.where(s < count, value, jnp.zeros_like(value))


def half_solve(level, received, column, infos, right, inverse, packed):
    slots, rows, order = right.shape[2:]
    return pl.pallas_call(
        functools.partial(half_kernel, level),
        out_shape=jax.ShapeDtypeStruct((CORES * slots, rows // CORES, order), jnp.float32),
        in_specs=[VMEM, SMEM, SMEM, SMEM, VMEM, VMEM, VMEM],
        out_specs=VMEM,
        compiler_params=PARAMS,
    )(received, column, *infos, right, inverse, packed)


def last_kernel(level, received, column, info, right, inverse, first, *refs):
    mine, theirs, out = refs[: level - 1], refs[level - 1], refs[level]
    slots, rows = right.shape[2:4]
    half = rows // CORES
    peers = received.shape[0] // (CORES * slots)
    core = column[0] % CORES
    near = pl.multiple_of(core * half, half)
    away = pl.multiple_of((1 - core) * half, half)
    out[0, 0] = first[...]
    for index in range(1, level):
        for s in range(slots):
            out[index, 0, s, pl.ds(near, half), :] = mine[index - 1][s]
            out[index, 0, s, pl.ds(away, half), :] = theirs[index - 1, s]
    for s in range(slots):
        pieces = []
        for c in range(CORES):
            update = received[c * slots + s]
            for peer in range(1, peers):
                update = update + received[(peer * CORES + c) * slots + s]
            pieces.append(update)
        update = jnp.concatenate(pieces, axis=0)
        value = dot(right[level, 0, s] - update, inverse[level, 0, s])
        live = s < info[3 * level, 0]
        out[level, 0, s] = jnp.where(live, value, jnp.zeros_like(value))


def last_solve(received, column, info, right, inverse, first, mine, theirs):
    return pl.pallas_call(
        functools.partial(last_kernel, right.shape[0] - 1),
        out_shape=jax.ShapeDtypeStruct(right.shape, jnp.float32),
        in_specs=[VMEM, SMEM, SMEM] + [VMEM] * (4 + len(mine)),
        out_specs=VMEM,
        compiler_params=pltpu.CompilerParams(vmem_limit_bytes=60 * 1024 * 1024),
    )(received, column, info, right, inverse, first, *mine, theirs)


def edge_kernel(level, last, edges, cols, slots, column, *refs):
    infos, couplings, history = refs[:2], refs[2:4], refs[4 : 4 + level]
    out, products = refs[4 + level :]
    core, chip = column[0] % CORES, column[0] // CORES
    chips = cols // CORES
    target_row = (infos[0].shape[0] - 1) // 3
    for c in range(CORES):
        for e in range(edges):
            p = jnp.maximum(infos[c][level - 1, e], 0)
            where = (p // slots) % cols
            there = where // CORES
            other = ((where % CORES) != core).astype(jnp.int32)
            group = (chip + STRIDE - there % STRIDE) % STRIDE
            place = ((group * (chips // STRIDE) + there // STRIDE) * CORES + other) * slots
            place = place + p % slots
            source_level = p // (slots * cols)
            block = history[0][place]
            for index in range(1, level):
                block = jnp.where(source_level == index, history[index][place], block)
            products[c, e] = dot(block, couplings[c][level - 1, 0, e])
    out[...] = jnp.zeros_like(out)
    for c in range(CORES):
        owner = jnp.where(core == c, 0, 1) if last else c
        for e in range(edges):
            goal = infos[c][target_row + level - 1, e]
            live = (goal >= 0).astype(jnp.float32)
            goal = jnp.maximum(goal, 0)
            goal = ((goal // slots) * CORES + owner) * slots + goal % slots
            out[goal] = out[goal] + products[c, e] * live


def edge_terms(level, last, column, infos, couplings, history, row_total, cols, slots):
    edges = couplings[0].shape[2]
    rows, order = history[0].shape[1:]
    return pl.pallas_call(
        functools.partial(edge_kernel, level, last, edges, cols, slots),
        out_shape=jax.ShapeDtypeStruct((row_total * CORES * slots, rows, order), jnp.float32),
        in_specs=[SMEM] * 3 + [VMEM] * (2 + len(history)),
        out_specs=VMEM,
        scratch_shapes=[pltpu.VMEM((CORES, edges, rows, order), jnp.float32)],
        compiler_params=PARAMS,
    )(column, *infos, *couplings, *history)


def swap(x, cols):
    return lax.ppermute(x, "col", [(i, i ^ 1) for i in range(cols)])


def gather_far(solved, cols):
    far = [
        [CORES * (STRIDE * hi + lo) + core for hi in range(cols // CORES // STRIDE)]
        for lo in range(STRIDE)
        for core in range(CORES)
    ]
    return lax.all_gather(solved, "col", axis=0, tiled=False, axis_index_groups=far)


def gather_near(mine, cols):
    def shift(x, k):
        return lax.ppermute(x, "col", [(i, (i + CORES * k) % cols) for i in range(cols)])

    half = mine.shape[0] // 2
    below, above = shift(mine, 1), shift(mine, -1)
    low, high = shift(mine[:half], 2), shift(mine[half:], -2)
    same = jnp.concatenate([mine, below, low, high, above])
    return same.reshape((-1,) + same.shape[2:])


def split_rows(solved, core, cols):
    pairs = [[CORES * chip + core for core in range(CORES)] for chip in range(cols // CORES)]
    both = lax.all_gather(solved, "col", axis=0, tiled=False, axis_index_groups=pairs)
    half = both.shape[2] // CORES
    both = lax.dynamic_slice_in_dim(both, core * half, half, axis=2)
    both = jnp.where(core == 0, both, jnp.flip(both, axis=0))
    return both.reshape((-1,) + both.shape[2:])


def on_device(
    right_sides, inverse_blocks, coupling_blocks, slot_counts, edge_sources, edge_targets
):
    level_total, _, slots = right_sides.shape[:3]
    rows, cols = lax.axis_size("row"), lax.axis_size("col")
    column = lax.axis_index("col").astype(jnp.int32)
    counts = jnp.transpose(slot_counts, (1, 2, 0))
    chip_groups = [
        [row * cols + CORES * chip + core for row in range(rows) for core in range(CORES)]
        for chip in range(cols // CORES)
    ]
    edges = edge_sources.shape[2]
    first = first_solve(counts, right_sides, inverse_blocks)
    solved = split_rows(first, column % CORES, cols)
    column = column.reshape(1)
    history, halves = [], []
    for level in range(1, level_total):
        last = level + 1 == level_total
        mine = gather_far(solved, cols)
        if level == 1:
            coupling, right, inverse, sources, targets, live, mine = lax.optimization_barrier((
                coupling_blocks, right_sides, inverse_blocks, edge_sources, edge_targets,
                slot_counts, mine,
            ))
            couplings = (coupling_blocks, swap(coupling, cols))
            info = jnp.concatenate([
                sources[:, 0], targets[:, 0],
                jnp.broadcast_to(live[:, 0], (level_total, edges)),
            ])
            order = right.shape[-1]
            note = jnp.pad(
                info.astype(jnp.float32), ((0, -info.shape[0] % 8), (0, order - edges))
            )
            packed = swap(jnp.concatenate([
                right[1:-1].reshape(-1, order), inverse[1:-1].reshape(-1, order), note,
            ]), cols)
            other = packed[packed.shape[0] - note.shape[0] :].astype(jnp.int32)
            infos = (info, other[: info.shape[0], :edges])
        if last:
            *blocks, mine = lax.optimization_barrier((*[h[slots:] for h in halves], mine))
            theirs = swap(jnp.stack(blocks), cols)
        history.append(gather_near(mine, cols))
        terms = edge_terms(
            level, last, column, infos, couplings, history, rows, cols, slots
        )
        if last:
            terms, theirs = lax.optimization_barrier((terms, theirs))
            received = lax.all_to_all(
                terms, ("row", "col"), 0, 0, tiled=True, axis_index_groups=chip_groups
            )
            return last_solve(
                received, column, info, right_sides, inverse_blocks, first, halves, theirs
            )
        received = lax.all_to_all(terms, "row", 0, 0, tiled=True)
        solved = half_solve(
            level, received, column, infos, right_sides, inverse_blocks, packed
        )
        halves.append(solved)


def solution(mesh):
    return jax.shard_map(
        on_device,
        mesh=mesh,
        in_specs=(
            P(None, "row", "col", None, None),
            P(None, "row", "col", None, None),
            P(None, "row", "col", None, None),
            P(None, "row", "col"),
            P(None, "row", "col"),
            P(None, "row", "col"),
        ),
        out_specs=P(None, "row", "col", None, None),
        check_vma=False,
    )
```
